512 devices in a mesh: node: 64 (over z, x, core), dp: 8 (over y).
Axes of the slice: x: 4, y: 8, z: 8, core: 2. Of those that a mesh axis runs over, the one named last changes fastest.
Arguments:
- features: bfloat16 [65536, 128], P('node'), may hold values from -6 to 6
- history: bfloat16 [65536, 512], P('node'), may hold values from -5 to 5
- boundary: int32 [3072], P('node'), may hold values from 0 to 1023, as said below
- batch_ids: int32 [64, 8, 128], P('node', 'dp'), may hold values from 0 to 1023, as said below
- halo_ids: int32 [64, 8, 64, 32], P('node', 'dp'), may hold values from 0 to 47, as said below
- halo_len: int32 [64, 8, 64], P('node', 'dp'), may hold values from 0 to 32, as said below
- edges_inner: bfloat16 [64, 8, 128, 128], P('node', 'dp'), as said below
- edges_halo: bfloat16 [64, 8, 128, 2048], P('node', 'dp'), as said below
- input_weight: bfloat16 [128, 512], replicated, may hold values from -0.5 to 0.5
- weight_one: bfloat16 [512, 512], replicated, may hold values from -0.25 to 0.25
- weight_two: bfloat16 [512, 512], replicated, may hold values from -0.25 to 0.25
- cotangent: bfloat16 [64, 8, 128, 512], P('node', 'dp'), may hold values from -6 to 6
Outputs:
- new_history: bfloat16 [65536, 512], P('node')
- grad_input: float32 [128, 512], P('node', 'dp')
- grad_one: float32 [512, 512], P('node', 'dp')
- grad_two: float32 [512, 512], P('node', 'dp')
The draws below stay inside these ranges and needn't reach their ends.
Inputs may be any that keep to these rules, and one draw needn't show every extreme that they name: `boundary`: within each partition's block of 48 entries the row numbers are distinct; the largest one is always present. For each partition i, batch_ids[i] over all dp indices holds every local row number once. `halo_ids`: each list of 32 positions holds distinct values. `halo_len`: every batch has some source partition whose list is full. `edges_inner`: entries are zero or positive. `edges_halo`: entries are zero or positive.
All inputs are finite; a program needn't handle non-finite values.
Results may differ from the reference program's by a relative error of at most 0.02.
Values may be sent and summed in bfloat16 or wider, within the bound.
A program may use at most 64 MiB of HBM per device.

```python
import math
import jax
import jax.numpy as jnp
from jax import lax

D = 512
FEAT = 128
TOK_DEV = 128
HP = 32
BND = 48
HIST_DEV = 1024
HALO = 2048
N_NODE = 64
N_DP = 8


def draw_boundary(key, part):
    key = jax.random.fold_in(key, 1)

    def per_owner(owner_key):
        first_key, second_key = jax.random.split(owner_key)
        shuffled = jax.random.permutation(first_key, HIST_DEV - 1)[:BND - 1]
        row_list = jnp.concatenate([shuffled, jnp.full((1,), HIST_DEV - 1, shuffled.dtype)])
        return jax.random.permutation(second_key, row_list).astype(jnp.int32)
    key_list = jax.random.split(key, N_NODE)
    return jax.vmap(per_owner)(key_list).reshape(-1).astype(jnp.int32)


def draw_batch_ids(key, part):
    key = jax.random.fold_in(key, 2)

    def per_owner(owner_key):
        return jax.random.permutation(owner_key, HIST_DEV).reshape(N_DP, TOK_DEV).astype(jnp.int32)
    key_list = jax.random.split(key, N_NODE)
    return jax.vmap(per_owner)(key_list).astype(jnp.int32)


def draw_halo_ids(key, part):
    key = jax.random.fold_in(key, 3)

    def per_list(list_key):
        return jax.random.permutation(list_key, BND)[:HP].astype(jnp.int32)
    key_list = jax.random.split(key, N_NODE * N_DP * N_NODE)
    return jax.vmap(per_list)(key_list).reshape(N_NODE, N_DP, N_NODE, HP).astype(jnp.int32)


def draw_halo_len(key, part):
    key = jax.random.fold_in(key, 4)
    base_key, heat_key, full_key = jax.random.split(key, 3)
    heat = jax.random.randint(heat_key, (N_NODE,), 0, HP // 2 + 1)
    base = jax.random.randint(base_key, (N_NODE, N_DP, N_NODE), 0, HP + 1)
    counts = jnp.minimum(base + heat[None, None, :], HP)
    chosen = jax.random.randint(full_key, (N_NODE, N_DP, 1), 0, N_NODE)
    sources = jnp.arange(N_NODE)[None, None, :]
    return jnp.where(sources == chosen, HP, counts).astype(jnp.int32)


def draw_edges_inner(key, part):
    key = jax.random.fold_in(key, 5)
    keep_key, value_key = jax.random.split(key)
    shape = (N_NODE, N_DP, TOK_DEV, TOK_DEV)
    keep = jax.random.randint(keep_key, shape, 0, 8) == 0
    weights = jnp.exp(jax.random.uniform(value_key, shape, jnp.float32, math.log(0.1), math.log(10.0)))
    return jnp.where(keep, weights, 0.0).astype(jnp.bfloat16)


def draw_edges_halo(key, part):
    key = jax.random.fold_in(key, 6)
    keep_key, value_key = jax.random.split(key)
    shape = (N_NODE, N_DP, TOK_DEV, HALO)
    keep = jax.random.randint(keep_key, shape, 0, 32) == 0
    weights = jnp.exp(jax.random.uniform(value_key, shape, jnp.float32, math.log(0.1), math.log(10.0)))
    return jnp.where(keep, weights, 0.0).astype(jnp.bfloat16)


def steps_of(key, extent, cuts, low, top_value):
    gain, own = 1.0, jax.random.fold_in(key, 6)
    for dim, shards_of in cuts:
        steps = jnp.exp(jax.random.uniform(jax.random.fold_in(own, dim), (shards_of,), jnp.float32, low / len(cuts), top_value / len(cuts)))
        gain = gain * jnp.repeat(steps, extent[dim] // shards_of).reshape([-1 if axis == dim else 1 for axis in range(len(extent))])
    return gain


def centred(rng, extent, width, reach, cuts=(), held_as=jnp.bfloat16):
    drawn = jax.random.normal(rng, extent, jnp.float32) * width
    if len(cuts) > 0:
        drawn = steps_of(rng, extent, cuts, -0.22, 0.18) * drawn
    return jnp.clip(drawn, min=-reach, max=reach).astype(held_as)


def setup_inputs(seed: int = 0) -> dict:
    arg_keys = jax.random.split(jax.random.key(seed), 13)
    return {
        "features": centred(arg_keys[0], (N_NODE * HIST_DEV, FEAT), 1.0, 6.0, ((0, 64),)),
        "history": centred(arg_keys[1], (N_NODE * HIST_DEV, D), 0.7, 5.0, ((0, 64),)),
        "boundary": draw_boundary(jax.random.fold_in(arg_keys[12], 71), 0),
        "batch_ids": draw_batch_ids(jax.random.fold_in(arg_keys[12], 71), 0),
        "halo_ids": draw_halo_ids(jax.random.fold_in(arg_keys[12], 71), 0),
        "halo_len": draw_halo_len(jax.random.fold_in(arg_keys[12], 71), 0),
        "edges_inner": draw_edges_inner(jax.random.fold_in(arg_keys[12], 71), 0),
        "edges_halo": draw_edges_halo(jax.random.fold_in(arg_keys[12], 71), 0),
        "input_weight": centred(arg_keys[8], (FEAT, D), FEAT ** -0.5, 0.5),
        "weight_one": centred(arg_keys[9], (D, D), D ** -0.5, 0.25),
        "weight_two": centred(arg_keys[10], (D, D), D ** -0.5, 0.25),
        "cotangent": centred(arg_keys[11], (N_NODE, N_DP, TOK_DEV, D), 1.0, 6.0, ((0, 64), (1, 8))),
    }


RESIDUAL_SHARE = 0.1
BETA_ONE = math.log(1.5)
BETA_TWO = math.log(1.25)
GELU_SCALE = math.sqrt(2.0 / math.pi)
CUBIC_TERM = 0.044715

def gelu_slope(value):
    argument = GELU_SCALE * (value + CUBIC_TERM * value * value * value)
    tangent = jnp.tanh(argument)
    result = 0.5 * value * (1.0 + tangent)
    slopes = 0.5 * (1.0 + tangent) + 0.5 * value * (1.0 - tangent * tangent) * GELU_SCALE * (1.0 + 3.0 * CUBIC_TERM * value * value)
    return (result, slopes)

def matmul(left, right):
    return jnp.dot(left, right, preferred_element_type=jnp.float32)

def inner_rows(left, right):
    return lax.dot_general(left, right, (((0,), (0,)), ((), ())), preferred_element_type=jnp.float32)

def outer_cols(left, right):
    return lax.dot_general(left, right, (((1,), (1,)), ((), ())), preferred_element_type=jnp.float32)

def local_step(x_own, x_halo, y_halo, inner_edges, halo_edges, input_weight, weight_one, weight_two, cotan):
    half = jnp.bfloat16
    single = jnp.float32
    pre_own = matmul(x_own, input_weight)
    act_own, slope_own = gelu_slope(pre_own)
    first_own = act_own.astype(half)
    pre_halo = matmul(x_halo, input_weight)
    act_halo, slope_halo = gelu_slope(pre_halo)
    first_halo = act_halo.astype(half)
    degree = 1.0 + lax.optimization_barrier(jnp.sum(inner_edges.astype(single), axis=1, keepdims=True)) + lax.optimization_barrier(jnp.sum(halo_edges.astype(single), axis=1, keepdims=True))
    own_single = first_own.astype(single)
    mix_one = matmul(inner_edges, first_own) + matmul(halo_edges, first_halo) + own_single
    blend_one = ((1.0 - RESIDUAL_SHARE) * mix_one / degree + RESIDUAL_SHARE * own_single).astype(half)
    pre_one = (1.0 - BETA_ONE) * blend_one.astype(single) + BETA_ONE * matmul(blend_one, weight_one)
    act_one, slope_one = gelu_slope(pre_one)
    new_rows = act_one.astype(half)
    mix_two = matmul(inner_edges, new_rows) + matmul(halo_edges, y_halo) + new_rows.astype(single)
    blend_two = ((1.0 - RESIDUAL_SHARE) * mix_two / degree + RESIDUAL_SHARE * own_single).astype(half)
    pre_two = (1.0 - BETA_TWO) * blend_two.astype(single) + BETA_TWO * matmul(blend_two, weight_two)
    act_two, slope_two = gelu_slope(pre_two)
    back_two = cotan.astype(single) * slope_two
    back_two_half = back_two.astype(half)
    grad_two = BETA_TWO * inner_rows(blend_two, back_two_half)
    back_blend_two = (1.0 - BETA_TWO) * back_two + BETA_TWO * outer_cols(back_two_half, weight_two)
    back_mix_two = ((1.0 - RESIDUAL_SHARE) * back_blend_two / degree).astype(half)
    back_fresh = back_mix_two.astype(single) + inner_rows(inner_edges, back_mix_two)
    back_one = back_fresh * slope_one
    back_one_half = back_one.astype(half)
    grad_one = BETA_ONE * inner_rows(blend_one, back_one_half)
    back_blend_one = (1.0 - BETA_ONE) * back_one + BETA_ONE * outer_cols(back_one_half, weight_one)
    back_mix_one = ((1.0 - RESIDUAL_SHARE) * back_blend_one / degree).astype(half)
    back_own = RESIDUAL_SHARE * (back_blend_one + back_blend_two) + back_mix_one.astype(single) + inner_rows(inner_edges, back_mix_one)
    back_halo = inner_rows(halo_edges, back_mix_one)
    pre_grad_own = (back_own * slope_own).astype(half)
    pre_grad_halo = (back_halo * slope_halo).astype(half)
    grad_in = inner_rows(x_own, pre_grad_own) + inner_rows(x_halo, pre_grad_halo)
    return (new_rows, grad_in, grad_one, grad_two)

def reference(features, history, boundary, batch_ids, halo_ids, halo_len, edges_inner, edges_halo, input_weight, weight_one, weight_two, cotangent):
    owners = jnp.arange(N_NODE, dtype=jnp.int32)
    slot_index = jnp.arange(HP, dtype=jnp.int32)

    def visit(carry, device):
        node_index = device // N_DP
        data_index = device % N_DP
        own_rows = batch_ids[node_index, data_index] + node_index * HIST_DEV
        x_own = features[own_rows]
        wanted = halo_ids[node_index, data_index]
        row_list = boundary[owners[:, None] * BND + wanted] + owners[:, None] * HIST_DEV
        row_list = row_list.reshape(-1).astype(jnp.int32)
        x_halo = features[row_list]
        y_halo = history[row_list]
        valid = (slot_index[None, :] < halo_len[node_index, data_index][:, None]).reshape(-1)
        halo_edges = jnp.where(valid[None, :], edges_halo[node_index, data_index], jnp.zeros((), edges_halo.dtype))
        new_rows, grad_in, grad_one, grad_two = local_step(x_own, x_halo, y_halo, edges_inner[node_index, data_index], halo_edges, input_weight, weight_one, weight_two, cotangent[node_index, data_index])
        total_in, total_one, total_two = carry
        return ((total_in + grad_in, total_one + grad_one, total_two + grad_two), new_rows)
    start = (jnp.zeros((FEAT, D), jnp.float32), jnp.zeros((D, D), jnp.float32), jnp.zeros((D, D), jnp.float32))
    devices = jnp.arange(N_NODE * N_DP, dtype=jnp.int32)
    totals, fresh_all = lax.scan(visit, start, devices)
    targets = (batch_ids + (owners * HIST_DEV)[:, None, None]).reshape(-1).astype(jnp.int32)
    new_history = history.at[targets].set(fresh_all.reshape(-1, D))
    grad_scale = (N_NODE * N_DP) ** (-0.5)
    return (new_history, totals[0] * grad_scale, totals[1] * grad_scale, totals[2] * grad_scale)
```

```python
import math

import jax
import jax.numpy as jnp
from jax import lax
from jax.experimental import pallas as pl
from jax.experimental.pallas import tpu as pltpu
from jax.sharding import PartitionSpec as P

RESIDUAL_SHARE = 0.1
BETA_ONE = math.log(1.5)
BETA_TWO = math.log(1.25)
GELU_SCALE = math.sqrt(2.0 / math.pi)
CUBIC_TERM = 0.044715

Z, X, C, Y = 8, 4, 2, 8
D, FEAT, TOK, HP, BND, ROWS = 512, 128, 128, 32, 48, 1024
HALF = D // 2
GROUP = X * C
COLS = GROUP * BND
SLOTS = GROUP * HP

F32 = jnp.float32
BF16 = jnp.bfloat16


def gelu(v):
    vv = v * v
    half = 0.5 + 0.5 * jnp.tanh(v * (GELU_SCALE + (GELU_SCALE * CUBIC_TERM) * vv))
    return v * half


def gelu_slope(v):
    vv = v * v
    half = 0.5 + 0.5 * jnp.tanh(v * (GELU_SCALE + (GELU_SCALE * CUBIC_TERM) * vv))
    g = v * half
    rise = (2.0 * GELU_SCALE) + (6.0 * GELU_SCALE * CUBIC_TERM) * vv
    return g, half + (g * (1.0 - half)) * rise


def mm(a, b):
    return lax.dot_general(a, b, (((1,), (0,)), ((), ())), preferred_element_type=F32)


def mm_tn(a, b):
    return lax.dot_general(a, b, (((0,), (0,)), ((), ())), preferred_element_type=F32)


def mm_nt(a, b):
    return lax.dot_general(a, b, (((1,), (1,)), ((), ())), preferred_element_type=F32)


def kernel(
    feat, hist, bnd, ids, wanted, inner, edges, w0, w1, w2, cot,
    new_hist, out0, out1, out2,
    xt, yt, e, slope, place, fresh_all, ids_all,
    gh, tmine, tsend, tcore, xsend, xrecv, zown, zsend, zrecv,
    qacc, qsend, qcore, qown, qzsend, qzrecv, qx, qxrecv, ysend, yrecv,
    ag_s, ag_r, fr_s, fr_r, id_s, id_r, rs_s, rs_r, qs_s, qs_r, y_s, y_r,
):
    node = lax.axis_index("node")
    y = lax.axis_index("dp")
    c = lax.rem(node, C)
    x = lax.rem(lax.div(node, C), X)
    z = lax.div(node, C * X)

    def wrap(v, n):
        return lax.rem(v + n, n)

    def node_of(zz, xx, cc):
        return (zz * X + xx) * C + cc

    def push(src, dst, ssem, rsem, to_node, to_y):
        return pltpu.make_async_remote_copy(
            src_ref=src, dst_ref=dst, send_sem=ssem, recv_sem=rsem,
            device_id=(to_node, to_y), device_id_type=pl.DeviceIdType.MESH,
        )

    barrier = pltpu.get_barrier_semaphore()
    peers = [(node_of(z, x, 1 - c), y)]
    peers += [(node_of(z, wrap(x + d, X), c), y) for d in range(1, X)]
    peers += [(node_of(wrap(z + d, Z), x, c), y) for d in range(1, Z)]
    peers += [(node_of(z, x, cc), wrap(y + d, Y)) for d in range(1, Y) for cc in range(C)]
    for to_node, to_y in peers:
        pl.semaphore_signal(barrier, inc=1, device_id=(to_node, to_y), device_id_type=pl.DeviceIdType.MESH)

    row_of = lax.broadcasted_iota(jnp.int32, (ROWS, BND), 0)
    pick = jnp.where(row_of == bnd[...], 1.0, 0.0).astype(BF16)
    xt[z, x, c] = mm_tn(pick, feat[...]).astype(BF16)
    yt[z, x, c] = mm_tn(pick, hist[...]).astype(BF16)
    ids_all[y] = jnp.broadcast_to(ids[...], (8, TOK))

    pl.semaphore_wait(barrier, len(peers))

    id_copies = [
        push(ids_all.at[y], ids_all.at[y], id_s.at[d - 1], id_r.at[d - 1], node, wrap(y + d, Y))
        for d in range(1, Y)
    ]
    for cp in id_copies:
        cp.start()

    tabs = (xt, yt)
    sibling = node_of(z, x, 1 - c)

    def zrel(r):
        if r < 4:
            return wrap(z - r, Z)
        return wrap(z + (r - 3), Z)

    def gather_copy(t, ref, idx, to_node):
        return push(ref, ref, ag_s.at[t, idx], ag_r.at[t, idx], to_node, y)

    up_z, down_z = node_of(wrap(z + 1, Z), x, c), node_of(wrap(z - 1, Z), x, c)
    up_x, down_x = node_of(z, wrap(x + 1, X), c), node_of(z, wrap(x - 1, X), c)

    def gather_even():
        sent = []

        def send(t, ref, idx, to_node):
            cp = gather_copy(t, ref, idx, to_node)
            cp.start()
            sent.append(cp)

        def arrived(t, ref, idx):
            gather_copy(t, ref, idx, sibling).wait_recv()

        def row(t, r):
            return tabs[t].at[zrel(r), :, 0]

        for t in range(2):
            for d in range(1, X):
                send(t, tabs[t].at[z, x, 0], d - 1, node_of(z, wrap(x + d, X), 0))
        for t in range(2):
            for d in range(1, X):
                arrived(t, tabs[t].at[z, wrap(x - d, X), 0], d - 1)
            send(t, row(t, 0), 3, up_z)
            send(t, row(t, 0), 7, down_z)
            send(t, row(t, 0), 11, sibling)
        for k in range(1, 4):
            for t in range(2):
                arrived(t, row(t, k), 2 + k)
                if k < 3:
                    send(t, row(t, k), 3 + k, up_z)
                else:
                    send(t, tabs[t].at[zrel(3), 0:2, 0], 6, up_z)
                send(t, row(t, k), 11 + k, sibling)
                arrived(t, row(t, 3 + k), 6 + k)
                if k < 3:
                    send(t, row(t, 3 + k), 7 + k, down_z)
                else:
                    send(t, tabs[t].at[zrel(6), 2:4, 0], 10, down_z)
                send(t, row(t, 3 + k), 14 + k, sibling)
        for t in range(2):
            arrived(t, tabs[t].at[zrel(7), 0:2, 0], 6)
            arrived(t, tabs[t].at[zrel(7), 2:4, 0], 10)
            send(t, row(t, 7), 18, sibling)
        for t in range(2):
            for r in range(Z):
                arrived(t, tabs[t].at[zrel(r), :, 1], 11 + r)
        for cp in sent:
            cp.wait_send()

    def gather_odd():
        sent = []

        def send(t, ref, idx, to_node):
            cp = gather_copy(t, ref, idx, to_node)
            cp.start()
            sent.append(cp)

        def arrived(t, ref, idx):
            gather_copy(t, ref, idx, sibling).wait_recv()

        def one(t, r, xx):
            return tabs[t].at[zrel(r), xx, 1]

        for t in range(2):
            send(t, one(t, 0, x), 3, up_z)
            send(t, one(t, 0, x), 7, down_z)
            send(t, one(t, 0, x), 20, up_x)
            send(t, one(t, 0, x), 28, down_x)
        for k in range(1, 4):
            for t in range(2):
                arrived(t, one(t, k, x), 2 + k)
                if k < 3:
                    send(t, one(t, k, x), 3 + k, up_z)
                else:
                    send(t, tabs[t].at[zrel(3), x, 1, 0:32], 6, up_z)
                send(t, one(t, k, x), 20 + k, up_x)
                send(t, one(t, k, x), 28 + k, down_x)
                arrived(t, one(t, 3 + k, x), 6 + k)
                if k < 3:
                    send(t, one(t, 3 + k, x), 7 + k, down_z)
                else:
                    send(t, tabs[t].at[zrel(6), x, 1, 32:48], 10, down_z)
                send(t, one(t, 3 + k, x), 23 + k, up_x)
                send(t, one(t, 3 + k, x), 31 + k, down_x)
        for t in range(2):
            arrived(t, tabs[t].at[zrel(7), x, 1, 0:32], 6)
            arrived(t, tabs[t].at[zrel(7), x, 1, 32:48], 10)
            send(t, one(t, 7, x), 27, up_x)
            send(t, one(t, 7, x), 35, down_x)
        left, right, far = wrap(x - 1, X), wrap(x + 1, X), wrap(x + 2, X)
        order = (0, 1, 4, 2, 5, 3, 6, 7)
        for r in order:
            for t in range(2):
                arrived(t, one(t, r, left), 20 + r)
                arrived(t, one(t, r, right), 28 + r)
                if r % 2 == 0:
                    send(t, one(t, r, left), 36 + r, up_x)
                else:
                    send(t, one(t, r, right), 36 + r, down_x)
        for r in order:
            for t in range(2):
                arrived(t, one(t, r, far), 36 + r)
                send(t, tabs[t].at[zrel(r), :, 1], 11 + r, sibling)
        for t in range(2):
            for r in range(Z):
                arrived(t, tabs[t].at[zrel(r), :, 0], 11 + r)
        for cp in sent:
            cp.wait_send()

    @pl.when(c == 0)
    def _():
        gather_even()

    @pl.when(c == 1)
    def _():
        gather_odd()

    r_i = lax.broadcasted_iota(jnp.int32, (COLS, SLOTS), 0)
    s_i = lax.broadcasted_iota(jnp.int32, (COLS, SLOTS), 1)
    target = jnp.where(lax.div(r_i, BND) == lax.div(s_i, HP), lax.rem(r_i, BND), -2)
    degree = 1.0 + jnp.sum(inner[...].astype(F32), axis=1, keepdims=True)
    for g in range(Z):
        spread = jnp.where(wanted[g:g + 1, :] == target, 1.0, 0.0).astype(BF16)
        part = mm_nt(edges[:, g * SLOTS:(g + 1) * SLOTS], spread)
        degree = degree + jnp.sum(part, axis=1, keepdims=True)
        e[g] = part.astype(BF16)
    scale = (1.0 - RESIDUAL_SHARE) / degree

    row_of = lax.broadcasted_iota(jnp.int32, (ROWS, TOK), 0)
    place[y] = jnp.where(row_of == ids[...], 1.0, 0.0).astype(BF16)
    x_own = mm_tn(place[y], feat[...]).astype(BF16)
    h_own, slope_own = gelu_slope(mm(x_own, w0[...]))
    h_own = h_own.astype(BF16)
    own = h_own.astype(F32)

    def layer_one(g, total):
        h, s = gelu_slope(mm(xt[g].reshape(COLS, FEAT), w0[...]))
        slope[g] = s
        return total + mm(e[g], h.astype(BF16))

    mix = lax.fori_loop(0, Z, layer_one, mm(inner[...], h_own) + own)
    s1 = (mix * scale + RESIDUAL_SHARE * own).astype(BF16)
    z1 = (1.0 - BETA_ONE) * s1.astype(F32) + BETA_ONE * mm(s1, w1[...])
    fresh, slope_one = gelu_slope(z1)
    fresh = fresh.astype(BF16)

    fresh_all[y] = fresh
    up_y, down_y = wrap(y + 1, Y), wrap(y - 1, Y)
    fresh_sent = []

    def fresh_send(block, rows, idx, to_y):
        ref = fresh_all.at[block, rows[0]:rows[1]]
        cp = push(ref, ref, fr_s.at[idx], fr_r.at[idx], node, to_y)
        cp.start()
        fresh_sent.append(cp)

    def fresh_arrived(block, rows, idx):
        ref = fresh_all.at[block, rows[0]:rows[1]]
        push(ref, ref, fr_s.at[idx], fr_r.at[idx], node, up_y).wait_recv()

    whole, low, high = (0, TOK), (0, TOK // 2), (TOK // 2, TOK)
    fresh_send(y, whole, 0, up_y)
    fresh_send(y, whole, 4, down_y)

    def fresh_step(k):
        below, above = wrap(y - k, Y), wrap(y + k, Y)
        if k < 4:
            fresh_arrived(below, whole, k - 1)
            fresh_send(below, whole if k < 3 else low, k, up_y)
            fresh_arrived(above, whole, 3 + k)
            fresh_send(above, whole if k < 3 else high, 4 + k, down_y)
        else:
            fresh_arrived(below, low, 3)
            fresh_arrived(above, high, 7)

    mix = mm(inner[...], fresh) + fresh.astype(F32)

    def layer_two(g, total):
        return total + mm(e[g], yt[g].reshape(COLS, D))

    mix = lax.fori_loop(0, Z, layer_two, mix)
    s2 = (mix * scale + RESIDUAL_SHARE * own).astype(BF16)
    z2 = (1.0 - BETA_TWO) * s2.astype(F32) + BETA_TWO * mm(s2, w2[...])
    _, slope_two = gelu_slope(z2)
    g2 = cot[...].astype(F32) * slope_two
    g2b = g2.astype(BF16)

    def term_start(m, s, gb, beta):
        gh[0] = gb[:, :HALF]
        gh[1] = gb[:, HALF:]
        tsend[m] = (beta * mm_tn(s, gh[1 - c])).astype(BF16).reshape(Z, X, 16, HALF)
        cp = push(tsend.at[m], tcore.at[m], rs_s.at[m, 0], rs_r.at[m, 0], sibling, y)
        cp.start()
        tmine[m] = (beta * mm_tn(s, gh[c])).reshape(Z, X, 16, HALF)
        return cp

    def term_x(m, core_copy):
        core_copy.wait()
        tmine[m] = tmine[m] + tcore[m].astype(F32)
        xsend[m] = tmine[m].astype(BF16)
        copies = []
        for d in range(1, X):
            to = wrap(x + d, X)
            cp = push(xsend.at[m, :, to], xrecv.at[m, d - 1], rs_s.at[m, d], rs_r.at[m, d], node_of(z, to, c), y)
            cp.start()
            copies.append(cp)
        return copies

    def term_z(m, x_copies):
        for cp in x_copies:
            cp.wait()
        total = tmine[m, :, x]
        for d in range(1, X):
            total = total + xrecv[m, d - 1].astype(F32)
        zown[m] = total
        zsend[m] = total.astype(BF16)
        copies = []
        for d in range(1, Z):
            to = wrap(z + d, Z)
            cp = push(
                zsend.at[m, to], zrecv.at[m, d - 1], rs_s.at[m, 3 + d], rs_r.at[m, 3 + d], node_of(to, x, c), y
            )
            cp.start()
            copies.append(cp)
        return copies

    def term_done(m, z_copies):
        for cp in z_copies:
            cp.wait()
        total = zown[m, z]
        for d in range(1, Z):
            total = total + zrecv[m, d - 1].astype(F32)
        return total

    two = term_start(1, s2, g2b, BETA_TWO)
    e2 = (1.0 - BETA_TWO) * g2 + BETA_TWO * mm_nt(g2b, w2[...])
    m2 = (e2 * scale).astype(BF16)
    g1 = (m2.astype(F32) + mm_tn(inner[...], m2)) * slope_one
    g1b = g1.astype(BF16)
    two = term_x(1, two)
    one = term_start(0, s1, g1b, BETA_ONE)
    fresh_step(1)
    e1 = (1.0 - BETA_ONE) * g1 + BETA_ONE * mm_nt(g1b, w1[...])
    m1 = (e1 * scale).astype(BF16)
    back_own = RESIDUAL_SHARE * (e1 + e2) + m1.astype(F32) + mm_tn(inner[...], m1)
    q_own = (back_own * slope_own).astype(BF16)
    one = term_x(0, one)

    def input_term(g, total):
        q = (mm_tn(e[g], m1) * slope[g]).astype(BF16)
        return total + mm_tn(xt[g].reshape(COLS, FEAT), q)

    t0 = lax.fori_loop(0, Z, input_term, mm_tn(x_own, q_own))
    qacc[0] = t0[:, :HALF]
    qacc[1] = t0[:, HALF:]

    qsend[...] = qacc[1 - c].astype(BF16)
    q_core = push(qsend, qcore, qs_s.at[0], qs_r.at[0], sibling, y)
    q_core.start()
    fresh_step(2)
    two = term_z(1, two)
    q_core.wait()
    total = (qacc[c] + qcore[...].astype(F32)).reshape(Z, 16, HALF)
    qown[...] = total
    qzsend[...] = total.astype(BF16)
    q_z = []
    for d in range(1, Z):
        to = wrap(z + d, Z)
        cp = push(qzsend.at[to], qzrecv.at[d - 1], qs_s.at[d], qs_r.at[d], node_of(to, x, c), y)
        cp.start()
        q_z.append(cp)
    one = term_z(0, one)
    fresh_step(3)
    r2 = term_done(1, two)
    for cp in q_z:
        cp.wait()
    total = qown[z]
    for d in range(1, Z):
        total = total + qzrecv[d - 1].astype(F32)
    qx[...] = total
    q_x = []
    for d in range(1, X):
        cp = push(qx, qxrecv.at[d - 1], qs_s.at[7 + d], qs_r.at[7 + d], node_of(z, wrap(x + d, X), c), y)
        cp.start()
        q_x.append(cp)
    r1 = term_done(0, one)
    for cp in q_x:
        cp.wait()
    r0 = qx[...]
    for d in range(1, X):
        r0 = r0 + qxrecv[d - 1]

    def columns(r, j):
        part = r[:, (j // 2) * 128:(j // 2) * 128 + 128]
        return part if j % 2 == 0 else pltpu.roll(part, 64, 1)

    per_core = Y // C
    me_y = lax.div(y, per_core)
    for j in range(per_core):
        a1, a2, a0 = columns(r1, j), columns(r2, j), columns(r0, j)
        for cc in range(C):
            ysend[j, cc, 0:8] = a1[cc * 8:cc * 8 + 8]
            ysend[j, cc, 8:16] = a2[cc * 8:cc * 8 + 8]
            ysend[j, cc, 16:24] = pltpu.roll(a0, lax.rem(16 - (x * 4 + cc * 2), 16), 0)[0:8]

    def y_copy(j, cc):
        return push(
            ysend.at[j, cc], yrecv.at[y], y_s.at[j * C + cc], y_r.at[y], node_of(z, x, cc), c * per_core + j
        )

    for j in range(per_core):
        for cc in range(C):
            mine = (c * per_core + j == y) & (c == cc)

            @pl.when(jnp.logical_not(mine))
            def _():
                y_copy(j, cc).start()

            @pl.when(mine)
            def _():
                yrecv[y] = ysend[j, cc]

    fresh_step(4)
    for cp in id_copies:
        cp.wait()
    row_of = lax.broadcasted_iota(jnp.int32, (ROWS, TOK), 0)
    rows = jnp.zeros((ROWS, D), F32)
    for yy in range(Y):
        put = jnp.where(row_of == ids_all[yy, 0:1], 1.0, 0.0).astype(BF16)
        rows = rows + mm(put, fresh_all[yy])
    new_hist[...] = rows.astype(BF16)

    for yy in range(Y):
        @pl.when(jnp.logical_not((yy == y) & (me_y == c)))
        def _():
            push(
                ysend.at[0, 0], yrecv.at[yy], y_s.at[0], y_r.at[yy], node, up_y
            ).wait_recv()
    total = yrecv[0]
    for yy in range(1, Y):
        total = total + yrecv[yy]
    total = total * ((Z * X * C * Y) ** (-0.5))
    out1[...] = total[0:8, 0:64]
    out2[...] = total[8:16, 0:64]
    out0[...] = total[16:18, 0:64]

    for cp in fresh_sent:
        cp.wait_send()
    for j in range(per_core):
        for cc in range(C):
            mine = (c * per_core + j == y) & (c == cc)

            @pl.when(jnp.logical_not(mine))
            def _():
                y_copy(j, cc).wait_send()


def per_device(
    features, history, boundary, batch_ids, halo_ids, halo_len, edges_inner, edges_halo,
    input_weight, weight_one, weight_two, cotangent,
):
    slot = jnp.arange(HP, dtype=jnp.int32)
    wanted = jnp.where(slot[None, :] < halo_len[0, 0][:, None], halo_ids[0, 0], -1).reshape(Z, SLOTS)
    vmem = pl.BlockSpec(memory_space=pltpu.VMEM)
    dma = pltpu.SemaphoreType.DMA
    outs = pl.pallas_call(
        kernel,
        out_shape=(
            jax.ShapeDtypeStruct((ROWS, D), BF16),
            jax.ShapeDtypeStruct((2, 64), F32),
            jax.ShapeDtypeStruct((8, 64), F32),
            jax.ShapeDtypeStruct((8, 64), F32),
        ),
        in_specs=[vmem] * 11,
        out_specs=(vmem,) * 4,
        scratch_shapes=[
            pltpu.VMEM((Z, X, C, BND, FEAT), BF16),
            pltpu.VMEM((Z, X, C, BND, D), BF16),
            pltpu.VMEM((Z, TOK, COLS), BF16),
            pltpu.VMEM((Z, COLS, D), F32),
            pltpu.VMEM((Y, ROWS, TOK), BF16),
            pltpu.VMEM((Y, TOK, D), BF16),
            pltpu.VMEM((Y, 8, TOK), jnp.int32),
            pltpu.VMEM((2, TOK, HALF), BF16),
            pltpu.VMEM((2, Z, X, 16, HALF), F32),
            pltpu.VMEM((2, Z, X, 16, HALF), BF16),
            pltpu.VMEM((2, Z, X, 16, HALF), BF16),
            pltpu.VMEM((2, Z, X, 16, HALF), BF16),
            pltpu.VMEM((2, X - 1, Z, 16, HALF), BF16),
            pltpu.VMEM((2, Z, 16, HALF), F32),
            pltpu.VMEM((2, Z, 16, HALF), BF16),
            pltpu.VMEM((2, Z - 1, 16, HALF), BF16),
            pltpu.VMEM((2, FEAT, HALF), F32),
            pltpu.VMEM((FEAT, HALF), BF16),
            pltpu.VMEM((FEAT, HALF), BF16),
            pltpu.VMEM((Z, 16, HALF), F32),
            pltpu.VMEM((Z, 16, HALF), BF16),
            pltpu.VMEM((Z - 1, 16, HALF), BF16),
            pltpu.VMEM((16, HALF), F32),
            pltpu.VMEM((X - 1, 16, HALF), F32),
            pltpu.VMEM((Y // C, C, 24, 128), F32),
            pltpu.VMEM((Y, 24, 128), F32),
            dma((2, 44)),
            dma((2, 44)),
            dma((8,)),
            dma((8,)),
            dma((Y - 1,)),
            dma((Y - 1,)),
            dma((2, 11)),
            dma((2, 11)),
            dma((11,)),
            dma((11,)),
            dma((8,)),
            dma((8,)),
        ],
        compiler_params=pltpu.CompilerParams(
            collective_id=0, has_side_effects=True, vmem_limit_bytes=48 * 1024 * 1024
        ),
        name="gcn_step",
    )(
        features, history, boundary.reshape(1, BND), batch_ids.reshape(1, TOK), wanted,
        edges_inner.reshape(TOK, TOK), edges_halo.reshape(TOK, Z * SLOTS),
        input_weight, weight_one, weight_two, cotangent.reshape(TOK, D),
    )
    return outs


def solution(mesh):
    return jax.shard_map(
        per_device,
        mesh=mesh,
        in_specs=(
            P("node", None),
            P("node", None),
            P("node"),
            P("node", "dp", None),
            P("node", "dp", None, None),
            P("node", "dp", None),
            P("node", "dp", None, None),
            P("node", "dp", None, None),
            P(),
            P(),
            P(),
            P("node", "dp", None, None),
        ),
        out_specs=(P("node", None), P("node", "dp"), P("node", "dp"), P("node", "dp")),
        check_vma=False,
    )
```

```python
import math

import jax
import jax.numpy as jnp
from jax import lax
from jax.experimental import pallas as pl
from jax.experimental.pallas import tpu as pltpu
from jax.sharding import PartitionSpec as P

RESIDUAL_SHARE = 0.1
BETA_ONE = math.log(1.5)
BETA_TWO = math.log(1.25)
GELU_SCALE = math.sqrt(2.0 / math.pi)
CUBIC_TERM = 0.044715

Z, X, C, Y = 8, 4, 2, 8
D, FEAT, TOK, HP, BND, ROWS = 512, 128, 128, 32, 48, 1024
HALF = D // 2
GROUP = X * C
COLS = GROUP * BND
SLOTS = GROUP * HP

F32 = jnp.float32
BF16 = jnp.bfloat16


def gelu(v):
    vv = v * v
    half = 0.5 + 0.5 * jnp.tanh(v * (GELU_SCALE + (GELU_SCALE * CUBIC_TERM) * vv))
    return v * half


def gelu_slope(v):
    vv = v * v
    half = 0.5 + 0.5 * jnp.tanh(v * (GELU_SCALE + (GELU_SCALE * CUBIC_TERM) * vv))
    g = v * half
    rise = (2.0 * GELU_SCALE) + (6.0 * GELU_SCALE * CUBIC_TERM) * vv
    return g, half + (g * (1.0 - half)) * rise


def mm(a, b):
    return lax.dot_general(a, b, (((1,), (0,)), ((), ())), preferred_element_type=F32)


def mm_tn(a, b):
    return lax.dot_general(a, b, (((0,), (0,)), ((), ())), preferred_element_type=F32)


def mm_nt(a, b):
    return lax.dot_general(a, b, (((1,), (1,)), ((), ())), preferred_element_type=F32)


def kernel(
    feat_in, hist_in, bnd_in, ids_in, halo_in, len_in, inner_in, edges_in, w0_in, w1_in, w2_in, cot_in,
    new_hist, out0, out1, out2,
    feat, hist, bnd, ids, halo, lens, inner, edges, w0, w1, w2, cot,
    xt, yt, e, slope, fresh_all, ids_all,
    gh, tmine, tsend, tcore, xsend, xrecv, zown, zsend, zrecv,
    qacc, qsend, qcore, qown, qzsend, qzrecv, qx, qxrecv, ysend, yrecv,
    in_s, f_s, f_r, h_s, h_r, fr_s, fr_r, id_s, id_r, rs_s, rs_r, qs_s, qs_r, y_s, y_r,
):
    node = lax.axis_index("node")
    y = lax.axis_index("dp")
    c = lax.rem(node, C)
    x = lax.rem(lax.div(node, C), X)
    z = lax.div(node, C * X)

    loads = {}
    for n, (name, src, dst) in enumerate((
        ("bnd", bnd_in, bnd), ("feat", feat_in, feat), ("hist", hist_in.at[:, pl.ds(pl.multiple_of(lax.rem(y, 2) * HALF, HALF), HALF)], hist), ("ids", ids_in.at[0], ids),
        ("halo", halo_in.at[0, 0], halo), ("len", len_in.at[0], lens), ("edges", edges_in.at[0, 0], edges),
        ("inner", inner_in.at[0, 0], inner), ("w0", w0_in, w0), ("w1", w1_in, w1), ("w2", w2_in, w2),
        ("cot", cot_in.at[0, 0], cot),
    )):
        loads[name] = pltpu.make_async_copy(src, dst, in_s.at[n])
        loads[name].start()

    def wrap(v, n):
        return lax.rem(v + n, n)

    def node_of(zz, xx, cc):
        return (zz * X + xx) * C + cc

    def push(src, dst, ssem, rsem, to_node, to_y):
        return pltpu.make_async_remote_copy(
            src_ref=src, dst_ref=dst, send_sem=ssem, recv_sem=rsem,
            device_id=(to_node, to_y), device_id_type=pl.DeviceIdType.MESH,
        )

    barrier = pltpu.get_barrier_semaphore()
    peers = [(node_of(z, x, 1 - c), y)]
    peers += [(node_of(z, wrap(x + d, X), c), y) for d in range(1, X)]
    peers += [(node_of(wrap(z + d, Z), x, c), y) for d in range(1, Z)]
    peers += [(node_of(z, x, cc), wrap(y + d, Y)) for d in range(1, Y) for cc in range(C)]
    for to_node, to_y in peers:
        pl.semaphore_signal(barrier, inc=1, device_id=(to_node, to_y), device_id_type=pl.DeviceIdType.MESH)

    side = lax.rem(y, 2)

    def lanes(start, size):
        return pl.ds(pl.multiple_of(start, 128), size)

    mine, others = side * HALF, (1 - side) * HALF
    row_of = lax.broadcasted_iota(jnp.int32, (ROWS, BND), 0)
    loads["bnd"].wait()
    pick = jnp.where(row_of == bnd[...].reshape(1, BND), 1.0, 0.0).astype(BF16)
    loads["feat"].wait()
    xt[z, x, c] = mm_tn(pick, feat[...]).astype(BF16)
    loads["ids"].wait()
    ids_all[y] = jnp.broadcast_to(ids[...], (8, TOK))

    pl.semaphore_wait(barrier, len(peers))

    sibling = node_of(z, x, 1 - c)

    def place_z(r, sign=1):
        if isinstance(r, int):
            step = (r + 1) // 2 if r % 2 == 1 else -(r // 2)
        else:
            far = lax.div(r + 1, 2)
            step = jnp.where(lax.rem(r, 2) == 1, far, -far)
        return wrap(z + sign * step, Z)

    def x_peer(k):
        return node_of(z, wrap(x + k + 1, X), c)

    def f_z(r):
        ref = xt.at[z, x, c]
        return push(ref, ref, f_s.at[r], f_r.at[r], node_of(place_z(r, -1), x, c), y)

    def f_z_in(r):
        ref = xt.at[place_z(r), x, c]
        return push(ref, ref, f_s.at[r], f_r.at[r], sibling, y)

    def f_x(r, k):
        ref = xt.at[place_z(r), x, c]
        return push(ref, ref, f_s.at[8 + 3 * r + k], f_r.at[8 + 3 * r + k], x_peer(k), y)

    def f_x_in(r, k):
        ref = xt.at[place_z(r), wrap(x - k - 1, X), c]
        return push(ref, ref, f_s.at[8 + 3 * r + k], f_r.at[8 + 3 * r + k], sibling, y)

    def f_core(r, core):
        ref = xt.at[place_z(r), :, core]
        return push(ref, ref, f_s.at[32 + r], f_r.at[32 + r], sibling, y)

    def h_z(r):
        ref = yt.at[z, x, c, :, lanes(mine, HALF)]
        return push(ref, ref, h_s.at[r], h_r.at[r], node_of(place_z(r, -1), x, c), y)

    def h_z_in(r):
        ref = yt.at[place_z(r), x, c, :, lanes(mine, HALF)]
        return push(ref, ref, h_s.at[r], h_r.at[r], sibling, y)

    def h_x(r, k):
        ref = yt.at[place_z(r), x, c, :, lanes(mine, HALF)]
        return push(ref, ref, h_s.at[8 + 3 * r + k], h_r.at[8 + 3 * r + k], x_peer(k), y)

    def h_x_in(r, k):
        ref = yt.at[place_z(r), wrap(x - k - 1, X), c, :, lanes(mine, HALF)]
        return push(ref, ref, h_s.at[8 + 3 * r + k], h_r.at[8 + 3 * r + k], sibling, y)

    def h_y(r, k):
        ref = yt.at[place_z(r), :, c, :, lanes(mine + 128 * k, 128)]
        return push(ref, ref, h_s.at[32 + 2 * r + k], h_r.at[32 + 2 * r + k], node, wrap(y + 1 - 2 * k, Y))

    def h_y_in(r, k):
        ref = yt.at[place_z(r), :, c, :, lanes(others + 128 * k, 128)]
        return push(ref, ref, h_s.at[32 + 2 * r + k], h_r.at[32 + 2 * r + k], sibling, y)

    def h_core(r, k, core):
        ref = yt.at[place_z(r), :, core, :, lanes(mine if k == 0 else others, HALF)]
        return push(ref, ref, h_s.at[48 + 2 * r + k], h_r.at[48 + 2 * r + k], sibling, y)

    for r in range(1, Z):
        f_z(r).start()
    for k in range(X - 1):
        f_x(0, k).start()
    loads["hist"].wait()
    yt[z, x, c, :, lanes(mine, HALF)] = mm_tn(pick, hist[...]).astype(BF16)
    for r in range(1, Z):
        h_z(r).start()

    id_copies = [
        push(ids_all.at[y], ids_all.at[y], id_s.at[d - 1], id_r.at[d - 1], node, wrap(y + d, Y))
        for d in range(1, Y)
    ]
    for cp in id_copies:
        cp.start()

    loads["len"].wait()
    loads["halo"].wait()
    slot = lax.broadcasted_iota(jnp.int32, (HP, Z * GROUP), 0)
    asked = jnp.where(slot < lens[...], halo[...], -1).astype(F32).astype(BF16)
    repeat = jnp.where(
        lax.rem(lax.broadcasted_iota(jnp.int32, (HP, SLOTS), 1), HP) == lax.broadcasted_iota(jnp.int32, (HP, SLOTS), 0),
        1.0, 0.0,
    ).astype(BF16)
    tiled = mm_tn(asked, repeat)
    in_list = lax.div(lax.broadcasted_iota(jnp.int32, (GROUP, SLOTS), 1), HP) == lax.broadcasted_iota(
        jnp.int32, (GROUP, SLOTS), 0
    )
    r_i = lax.broadcasted_iota(jnp.int32, (COLS, SLOTS), 0)
    s_i = lax.broadcasted_iota(jnp.int32, (COLS, SLOTS), 1)
    target = jnp.where(lax.div(r_i, BND) == lax.div(s_i, HP), lax.rem(r_i, BND), -2).astype(F32)
    loads["inner"].wait()
    degree = 1.0 + jnp.sum(inner[...].astype(F32), axis=1, keepdims=True)
    loads["edges"].wait()
    for g in range(Z):
        wanted = jnp.sum(jnp.where(in_list, tiled[g * GROUP:(g + 1) * GROUP], 0.0), axis=0, keepdims=True)
        spread = jnp.where(wanted == target, 1.0, 0.0).astype(BF16)
        part = mm_nt(edges[:, g * SLOTS:(g + 1) * SLOTS], spread)
        degree = degree + jnp.sum(part, axis=1, keepdims=True)
        e[g] = part.astype(BF16)
    scale = (1.0 - RESIDUAL_SHARE) / degree

    row_of = lax.broadcasted_iota(jnp.int32, (ROWS, TOK), 0)
    place = jnp.where(row_of == ids[...], 1.0, 0.0).astype(BF16)
    x_own = mm_tn(place, feat[...]).astype(BF16)
    loads["w0"].wait()
    h_own, slope_own = gelu_slope(mm(x_own, w0[...]))
    h_own = h_own.astype(BF16)
    own = h_own.astype(F32)
    mix = mm(inner[...], h_own) + own

    for r in range(1, Z):
        f_z_in(r).wait_recv()
        for k in range(X - 1):
            f_x(r, k).start()
    for r in range(Z):
        if r > 0:
            h_z_in(r).wait_recv()
        for k in range(X - 1):
            h_x(r, k).start()
    for r in range(Z):
        for k in range(X - 1):
            f_x_in(r, k).wait_recv()
        f_core(r, c).start()

    def layer_one(r, total):
        f_core(r, 1 - c).wait_recv()
        g = place_z(r)
        h, s = gelu_slope(mm(xt[g].reshape(COLS, FEAT), w0[...]))
        slope[g] = s
        total = total + mm(e[g], h.astype(BF16))
        for k in range(X - 1):
            h_x_in(r, k).wait_recv()
        h_y(r, 0).start()
        h_y(r, 1).start()
        h_core(r, 0, c).start()
        return total

    mix = lax.fori_loop(0, Z, layer_one, mix)
    s1 = (mix * scale + RESIDUAL_SHARE * own).astype(BF16)
    loads["w1"].wait()
    z1 = (1.0 - BETA_ONE) * s1.astype(F32) + BETA_ONE * mm(s1, w1[...])
    fresh, slope_one = gelu_slope(z1)
    fresh = fresh.astype(BF16)

    fresh_all[y] = fresh
    fresh_sent = []

    def fresh_copy(dy, idx, to, half=None):
        block = wrap(y + dy, Y)
        ref = fresh_all.at[block] if half is None else fresh_all.at[block, half * 64:half * 64 + 64]
        return push(ref, ref, fr_s.at[idx], fr_r.at[idx], node, wrap(y + to, Y))

    def fresh_send(*args):
        cp = fresh_copy(*args)
        cp.start()
        fresh_sent.append(cp)

    fresh_send(0, 2, 2)
    fresh_send(0, 3, -2)
    fresh_send(0, 0, 1)
    fresh_send(0, 1, -1)

    def fresh_pass():
        fresh_copy(-2, 2, 1).wait_recv()
        fresh_copy(2, 3, 1).wait_recv()
        fresh_send(-2, 6, 2, 0)
        fresh_send(2, 7, -2, 1)
        fresh_send(-2, 4, 1)
        fresh_send(2, 5, -1)

    def fresh_end():
        fresh_copy(-1, 0, 1).wait_recv()
        fresh_copy(1, 1, 1).wait_recv()
        fresh_copy(-3, 4, 1).wait_recv()
        fresh_copy(3, 5, 1).wait_recv()
        fresh_copy(-4, 6, 1, 0).wait_recv()
        fresh_copy(4, 7, 1, 1).wait_recv()

    mix = mm(inner[...], fresh) + fresh.astype(F32)

    def history_core(r, carry):
        h_y_in(r, 0).wait_recv()
        h_y_in(r, 1).wait_recv()
        h_core(r, 1, c).start()
        return carry

    lax.fori_loop(0, Z, history_core, 0)

    def layer_two(r, total):
        h_core(r, 0, 1 - c).wait_recv()
        h_core(r, 1, 1 - c).wait_recv()
        g = place_z(r)
        return total + mm(e[g], yt[g].reshape(COLS, D))

    mix = lax.fori_loop(0, Z, layer_two, mix)
    s2 = (mix * scale + RESIDUAL_SHARE * own).astype(BF16)
    loads["w2"].wait()
    z2 = (1.0 - BETA_TWO) * s2.astype(F32) + BETA_TWO * mm(s2, w2[...])
    _, slope_two = gelu_slope(z2)
    loads["cot"].wait()
    g2 = cot[...].astype(F32) * slope_two
    g2b = g2.astype(BF16)

    def term_start(m, s, gb, beta):
        gh[0] = gb[:, :HALF]
        gh[1] = gb[:, HALF:]
        tsend[m] = (beta * mm_tn(s, gh[1 - c])).astype(BF16).reshape(Z, X, 16, HALF)
        cp = push(tsend.at[m], tcore.at[m], rs_s.at[m, 0], rs_r.at[m, 0], sibling, y)
        cp.start()
        tmine[m] = (beta * mm_tn(s, gh[c])).reshape(Z, X, 16, HALF)
        return cp

    def term_x(m, core_copy):
        core_copy.wait()
        tmine[m] = tmine[m] + tcore[m].astype(F32)
        xsend[m] = tmine[m].astype(BF16)
        copies = []
        for d in range(1, X):
            to = wrap(x + d, X)
            cp = push(xsend.at[m, :, to], xrecv.at[m, d - 1], rs_s.at[m, d], rs_r.at[m, d], node_of(z, to, c), y)
            cp.start()
            copies.append(cp)
        return copies

    def term_z(m, x_copies):
        for cp in x_copies:
            cp.wait()
        total = tmine[m, :, x]
        for d in range(1, X):
            total = total + xrecv[m, d - 1].astype(F32)
        zown[m] = total
        zsend[m] = total.astype(BF16)
        copies = []
        for d in range(1, Z):
            to = wrap(z + d, Z)
            cp = push(
                zsend.at[m, to], zrecv.at[m, d - 1], rs_s.at[m, 3 + d], rs_r.at[m, 3 + d], node_of(to, x, c), y
            )
            cp.start()
            copies.append(cp)
        return copies

    def term_done(m, z_copies):
        for cp in z_copies:
            cp.wait()
        total = zown[m, z]
        for d in range(1, Z):
            total = total + zrecv[m, d - 1].astype(F32)
        return total

    two = term_start(1, s2, g2b, BETA_TWO)
    e2 = (1.0 - BETA_TWO) * g2 + BETA_TWO * mm_nt(g2b, w2[...])
    m2 = (e2 * scale).astype(BF16)
    g1 = (m2.astype(F32) + mm_tn(inner[...], m2)) * slope_one
    g1b = g1.astype(BF16)
    two = term_x(1, two)
    one = term_start(0, s1, g1b, BETA_ONE)
    e1 = (1.0 - BETA_ONE) * g1 + BETA_ONE * mm_nt(g1b, w1[...])
    m1 = (e1 * scale).astype(BF16)
    back_own = RESIDUAL_SHARE * (e1 + e2) + m1.astype(F32) + mm_tn(inner[...], m1)
    q_own = (back_own * slope_own).astype(BF16)
    one = term_x(0, one)

    def input_term(g, total):
        q = (mm_tn(e[g], m1) * slope[g]).astype(BF16)
        return total + mm_tn(xt[g].reshape(COLS, FEAT), q)

    t0 = lax.fori_loop(0, Z, input_term, mm_tn(x_own, q_own))
    qacc[0] = t0[:, :HALF]
    qacc[1] = t0[:, HALF:]

    qsend[...] = qacc[1 - c].astype(BF16)
    q_core = push(qsend, qcore, qs_s.at[0], qs_r.at[0], sibling, y)
    q_core.start()
    fresh_pass()
    two = term_z(1, two)
    q_core.wait()
    total = (qacc[c] + qcore[...].astype(F32)).reshape(Z, 16, HALF)
    qown[...] = total
    qzsend[...] = total.astype(BF16)
    q_z = []
    for d in range(1, Z):
        to = wrap(z + d, Z)
        cp = push(qzsend.at[to], qzrecv.at[d - 1], qs_s.at[d], qs_r.at[d], node_of(to, x, c), y)
        cp.start()
        q_z.append(cp)
    one = term_z(0, one)
    r2 = term_done(1, two)
    for cp in q_z:
        cp.wait()
    total = qown[z]
    for d in range(1, Z):
        total = total + qzrecv[d - 1].astype(F32)
    qx[...] = total
    q_x = []
    for d in range(1, X):
        cp = push(qx, qxrecv.at[d - 1], qs_s.at[7 + d], qs_r.at[7 + d], node_of(z, wrap(x + d, X), c), y)
        cp.start()
        q_x.append(cp)
    r1 = term_done(0, one)
    for cp in q_x:
        cp.wait()
    r0 = qx[...]
    for d in range(1, X):
        r0 = r0 + qxrecv[d - 1]

    def columns(r, j):
        part = r[:, (j // 2) * 128:(j // 2) * 128 + 128]
        return part if j % 2 == 0 else pltpu.roll(part, 64, 1)

    per_core = Y // C
    me_y = lax.div(y, per_core)
    for j in range(per_core):
        a1, a2, a0 = columns(r1, j), columns(r2, j), columns(r0, j)
        for cc in range(C):
            ysend[j, cc, 0:8] = a1[cc * 8:cc * 8 + 8]
            ysend[j, cc, 8:16] = a2[cc * 8:cc * 8 + 8]
            ysend[j, cc, 16:24] = pltpu.roll(a0, lax.rem(16 - (x * 4 + cc * 2), 16), 0)[0:8]

    def y_copy(j, cc):
        return push(
            ysend.at[j, cc], yrecv.at[y], y_s.at[j * C + cc], y_r.at[y], node_of(z, x, cc), c * per_core + j
        )

    for j in range(per_core):
        for cc in range(C):
            kept = (c * per_core + j == y) & (c == cc)

            @pl.when(jnp.logical_not(kept))
            def _():
                y_copy(j, cc).start()

            @pl.when(kept)
            def _():
                yrecv[y] = ysend[j, cc]

    fresh_end()
    for cp in id_copies:
        cp.wait()
    rows = jnp.zeros((ROWS, D), F32)
    for yy in range(Y):
        put = jnp.where(row_of == ids_all[yy, 0:1], 1.0, 0.0).astype(BF16)
        rows = rows + mm(put, fresh_all[yy])
    new_hist[...] = rows.astype(BF16)

    for yy in range(Y):
        @pl.when(jnp.logical_not((yy == y) & (me_y == c)))
        def _():
            push(
                ysend.at[0, 0], yrecv.at[yy], y_s.at[0], y_r.at[yy], node, wrap(y + 1, Y)
            ).wait_recv()
    total = yrecv[0]
    for yy in range(1, Y):
        total = total + yrecv[yy]
    total = total * ((Z * X * C * Y) ** (-0.5))
    out1[...] = total[0:8, 0:64]
    out2[...] = total[8:16, 0:64]
    out0[...] = total[16:18, 0:64]

    for cp in fresh_sent:
        cp.wait_send()

    def gather_sent(r, carry):
        for k in range(X - 1):
            f_x(r, k).wait_send()
            h_x(r, k).wait_send()
        f_core(r, c).wait_send()
        for k in range(2):
            h_y(r, k).wait_send()
            h_core(r, k, c).wait_send()
        return carry

    lax.fori_loop(0, Z, gather_sent, 0)
    for r in range(1, Z):
        f_z(r).wait_send()
        h_z(r).wait_send()
    for j in range(per_core):
        for cc in range(C):
            kept = (c * per_core + j == y) & (c == cc)

            @pl.when(jnp.logical_not(kept))
            def _():
                y_copy(j, cc).wait_send()


def write_out(a, b, c, d, a_out, b_out, c_out, d_out, sems):
    copies = [
        pltpu.make_async_copy(src, dst, sems.at[n])
        for n, (src, dst) in enumerate(((a, a_out), (b, b_out), (c, c_out), (d, d_out)))
    ]
    for cp in copies:
        cp.start()
    for cp in copies:
        cp.wait()


def per_device(
    features, history, boundary, batch_ids, halo_ids, halo_len, edges_inner, edges_halo,
    input_weight, weight_one, weight_two, cotangent,
):
    vmem = pl.BlockSpec(memory_space=pltpu.VMEM)
    anywhere = pl.BlockSpec(memory_space=pl.ANY)
    dma = pltpu.SemaphoreType.DMA
    results = (
        jax.ShapeDtypeStruct((ROWS, D), BF16),
        jax.ShapeDtypeStruct((2, 64), F32),
        jax.ShapeDtypeStruct((8, 64), F32),
        jax.ShapeDtypeStruct((8, 64), F32),
    )
    outs = pl.pallas_call(
        kernel,
        out_shape=results,
        in_specs=[anywhere] * 12,
        out_specs=(vmem,) * 4,
        scratch_shapes=[
            pltpu.VMEM((ROWS, FEAT), BF16),
            pltpu.VMEM((ROWS, HALF), BF16),
            pltpu.VMEM((BND,), jnp.int32),
            pltpu.VMEM((1, TOK), jnp.int32),
            pltpu.VMEM((HP, Z * GROUP), jnp.int32),
            pltpu.VMEM((1, Z * GROUP), jnp.int32),
            pltpu.VMEM((TOK, TOK), BF16),
            pltpu.VMEM((TOK, Z * SLOTS), BF16),
            pltpu.VMEM((FEAT, D), BF16),
            pltpu.VMEM((D, D), BF16),
            pltpu.VMEM((D, D), BF16),
            pltpu.VMEM((TOK, D), BF16),
            pltpu.VMEM((Z, X, C, BND, FEAT), BF16),
            pltpu.VMEM((Z, X, C, BND, D), BF16),
            pltpu.VMEM((Z, TOK, COLS), BF16),
            pltpu.VMEM((Z, COLS, D), F32),
            pltpu.VMEM((Y, TOK, D), BF16),
            pltpu.VMEM((Y, 8, TOK), jnp.int32),
            pltpu.VMEM((2, TOK, HALF), BF16),
            pltpu.VMEM((2, Z, X, 16, HALF), F32),
            pltpu.VMEM((2, Z, X, 16, HALF), BF16),
            pltpu.VMEM((2, Z, X, 16, HALF), BF16),
            pltpu.VMEM((2, Z, X, 16, HALF), BF16),
            pltpu.VMEM((2, X - 1, Z, 16, HALF), BF16),
            pltpu.VMEM((2, Z, 16, HALF), F32),
            pltpu.VMEM((2, Z, 16, HALF), BF16),
            pltpu.VMEM((2, Z - 1, 16, HALF), BF16),
            pltpu.VMEM((2, FEAT, HALF), F32),
            pltpu.VMEM((FEAT, HALF), BF16),
            pltpu.VMEM((FEAT, HALF), BF16),
            pltpu.VMEM((Z, 16, HALF), F32),
            pltpu.VMEM((Z, 16, HALF), BF16),
            pltpu.VMEM((Z - 1, 16, HALF), BF16),
            pltpu.VMEM((16, HALF), F32),
            pltpu.VMEM((X - 1, 16, HALF), F32),
            pltpu.VMEM((Y // C, C, 24, 128), F32),
            pltpu.VMEM((Y, 24, 128), F32),
            dma((12,)),
            dma((40,)),
            dma((40,)),
            dma((64,)),
            dma((64,)),
            dma((8,)),
            dma((8,)),
            dma((Y - 1,)),
            dma((Y - 1,)),
            dma((2, 11)),
            dma((2, 11)),
            dma((11,)),
            dma((11,)),
            dma((8,)),
            dma((8,)),
        ],
        compiler_params=pltpu.CompilerParams(
            collective_id=0, has_side_effects=True, vmem_limit_bytes=62 * 1024 * 1024
        ),
        name="gcn_step",
    )(
        features, history, boundary, batch_ids, jnp.swapaxes(halo_ids, 2, 3), halo_len, edges_inner, edges_halo,
        input_weight, weight_one, weight_two, cotangent,
    )
    return pl.pallas_call(
        write_out,
        out_shape=results,
        in_specs=[vmem] * 4,
        out_specs=(anywhere,) * 4,
        scratch_shapes=[dma((4,))],
        name="write_out",
    )(*outs)


def solution(mesh):
    return jax.shard_map(
        per_device,
        mesh=mesh,
        in_specs=(
            P("node", None),
            P("node", None),
            P("node"),
            P("node", "dp", None),
            P("node", "dp", None, None),
            P("node", "dp", None),
            P("node", "dp", None, None),
            P("node", "dp", None, None),
            P(),
            P(),
            P(),
            P("node", "dp", None, None),
        ),
        out_specs=(P("node", None), P("node", "dp"), P("node", "dp"), P("node", "dp")),
        check_vma=False,
    )
```

```python
import math

import jax
import jax.numpy as jnp
from jax import lax
from jax.experimental import pallas as pl
from jax.experimental.pallas import tpu as pltpu
from jax.sharding import PartitionSpec as P

RESIDUAL_SHARE = 0.1
BETA_ONE = math.log(1.5)
BETA_TWO = math.log(1.25)
GELU_SCALE = math.sqrt(2.0 / math.pi)
CUBIC_TERM = 0.044715

Z, X, C, Y = 8, 4, 2, 8
D, FEAT, TOK, HP, BND, ROWS = 512, 128, 128, 32, 48, 1024
HALF = D // 2
GROUP = X * C
COLS = GROUP * BND
SLOTS = GROUP * HP

FIRST, LAST = pl.ds(0, 32), pl.ds(32, 16)

F32 = jnp.float32
BF16 = jnp.bfloat16


def gelu(v):
    vv = v * v
    half = 0.5 + 0.5 * jnp.tanh(v * (GELU_SCALE + (GELU_SCALE * CUBIC_TERM) * vv))
    return v * half


def gelu_slope(v):
    vv = v * v
    half = 0.5 + 0.5 * jnp.tanh(v * (GELU_SCALE + (GELU_SCALE * CUBIC_TERM) * vv))
    g = v * half
    rise = (2.0 * GELU_SCALE) + (6.0 * GELU_SCALE * CUBIC_TERM) * vv
    return g, half + (g * (1.0 - half)) * rise


def mm(a, b):
    return lax.dot_general(a, b, (((1,), (0,)), ((), ())), preferred_element_type=F32)


def mm_tn(a, b):
    return lax.dot_general(a, b, (((0,), (0,)), ((), ())), preferred_element_type=F32)


def mm_nt(a, b):
    return lax.dot_general(a, b, (((1,), (1,)), ((), ())), preferred_element_type=F32)


def kernel(
    feat_in, hist_in, bnd_in, ids_in, halo_in, len_in, inner_in, edges_in, w0_in, w1_in, w2_in, cot_in,
    new_hist, out0, out1, out2,
    feat, hist, bnd, ids, halo, lens, inner, edges, w0, w1, w2, cot,
    xt, yt, e, e_t, x_t, slope, fresh_all, ids_all,
    gh, tmine, tsend, tcore, xsend, xrecv, zown, zsend, zrecv,
    qacc, qsend, qcore, qown, qzsend, qzrecv, qx, qxrecv, ysend, yrecv,
    in_s, f_s, f_r, h_s, h_r, fr_s, fr_r, id_s, id_r, rs_s, rs_r, qs_s, qs_r, y_s, y_r,
):
    node = lax.axis_index("node")
    y = lax.axis_index("dp")
    c = lax.rem(node, C)
    x = lax.rem(lax.div(node, C), X)
    z = lax.div(node, C * X)

    loads = {}
    for n, (name, src, dst) in enumerate((
        ("bnd", bnd_in, bnd), ("feat", feat_in, feat), ("hist", hist_in.at[:, pl.ds(pl.multiple_of(lax.rem(y, 2) * HALF, HALF), HALF)], hist), ("ids", ids_in.at[0], ids),
        ("halo", halo_in.at[0, 0], halo), ("len", len_in.at[0], lens), ("edges", edges_in.at[0, 0], edges),
        ("inner", inner_in.at[0, 0], inner), ("w0", w0_in, w0), ("w1", w1_in, w1), ("w2", w2_in, w2),
        ("cot", cot_in.at[0, 0], cot),
    )):
        loads[name] = pltpu.make_async_copy(src, dst, in_s.at[n])
        loads[name].start()

    def wrap(v, n):
        return lax.rem(v + n, n)

    def node_of(zz, xx, cc):
        return (zz * X + xx) * C + cc

    def push(src, dst, ssem, rsem, to_node, to_y):
        return pltpu.make_async_remote_copy(
            src_ref=src, dst_ref=dst, send_sem=ssem, recv_sem=rsem,
            device_id=(to_node, to_y), device_id_type=pl.DeviceIdType.MESH,
        )

    barrier = pltpu.get_barrier_semaphore()
    far_first = (4, 3, 5, 2, 6, 1, 7)
    peers = [(node_of(wrap(z + d, Z), x, c), y) for d in far_first]
    peers += [(node_of(z, x, cc), wrap(y + d, Y)) for d in far_first for cc in range(C)]
    peers += [(node_of(z, wrap(x + d, X), c), y) for d in (2, 1, 3)]
    peers += [(node_of(z, x, 1 - c), y)]
    for to_node, to_y in peers:
        pl.semaphore_signal(barrier, inc=1, device_id=(to_node, to_y), device_id_type=pl.DeviceIdType.MESH)

    side = lax.rem(y, 2)

    def lanes(start, size):
        return pl.ds(pl.multiple_of(start, 128), size)

    mine, others = side * HALF, (1 - side) * HALF
    row_of = lax.broadcasted_iota(jnp.int32, (ROWS, BND), 0)
    loads["bnd"].wait()
    pick = jnp.where(row_of == bnd[...].reshape(1, BND), 1.0, 0.0).astype(BF16)
    loads["feat"].wait()
    xt[z, x, c] = mm_tn(pick, feat[...]).astype(BF16)
    loads["ids"].wait()
    ids_all[y] = jnp.broadcast_to(ids[...], (8, TOK))

    pl.semaphore_wait(barrier, len(peers))

    sibling = node_of(z, x, 1 - c)

    def place_z(r, sign=1):
        if isinstance(r, int):
            step = (r + 1) // 2 if r % 2 == 1 else -(r // 2)
        else:
            far = lax.div(r + 1, 2)
            step = jnp.where(lax.rem(r, 2) == 1, far, -far)
        return wrap(z + sign * step, Z)

    def x_peer(k):
        return node_of(z, wrap(x + k + 1, X), c)

    def f_z(r):
        ref = xt.at[z, x, c]
        return push(ref, ref, f_s.at[r], f_r.at[r], node_of(place_z(r, -1), x, c), y)

    def f_z_in(r):
        ref = xt.at[place_z(r), x, c]
        return push(ref, ref, f_s.at[r], f_r.at[r], sibling, y)

    def f_x(r, k):
        ref = xt.at[place_z(r), x, c]
        return push(ref, ref, f_s.at[8 + 3 * r + k], f_r.at[8 + 3 * r + k], x_peer(k), y)

    def f_x_in(r, k):
        ref = xt.at[place_z(r), wrap(x - k - 1, X), c]
        return push(ref, ref, f_s.at[8 + 3 * r + k], f_r.at[8 + 3 * r + k], sibling, y)

    def f_core(r, core):
        ref = xt.at[place_z(r), :, core]
        return push(ref, ref, f_s.at[32 + r], f_r.at[32 + r], sibling, y)

    def h_z(r):
        ref = yt.at[z, x, c, FIRST, lanes(mine, HALF)]
        return push(ref, ref, h_s.at[r], h_r.at[r], node_of(place_z(r, -1), x, c), y)

    def h_z_in(r):
        ref = yt.at[place_z(r), x, c, FIRST, lanes(mine, HALF)]
        return push(ref, ref, h_s.at[r], h_r.at[r], sibling, y)

    def h_x(r, k):
        ref = yt.at[place_z(r), x, c, FIRST, lanes(mine, HALF)]
        return push(ref, ref, h_s.at[8 + 3 * r + k], h_r.at[8 + 3 * r + k], x_peer(k), y)

    def h_x_in(r, k):
        ref = yt.at[place_z(r), wrap(x - k - 1, X), c, FIRST, lanes(mine, HALF)]
        return push(ref, ref, h_s.at[8 + 3 * r + k], h_r.at[8 + 3 * r + k], sibling, y)

    def l_x(k):
        ref = yt.at[z, x, c, LAST, lanes(mine, HALF)]
        return push(ref, ref, h_s.at[64 + k], h_r.at[64 + k], x_peer(k), y)

    def l_x_in(k):
        ref = yt.at[z, wrap(x - k - 1, X), c, LAST, lanes(mine, HALF)]
        return push(ref, ref, h_s.at[64 + k], h_r.at[64 + k], sibling, y)

    def l_z(r):
        ref = yt.at[z, :, c, LAST, lanes(mine, HALF)]
        return push(ref, ref, h_s.at[67 + r], h_r.at[67 + r], node_of(place_z(r, -1), x, c), y)

    def l_z_in(r):
        ref = yt.at[place_z(r), :, c, LAST, lanes(mine, HALF)]
        return push(ref, ref, h_s.at[67 + r], h_r.at[67 + r], sibling, y)

    def h_y(r, k):
        ref = yt.at[place_z(r), :, c, :, lanes(mine + 128 * k, 128)]
        return push(ref, ref, h_s.at[32 + 2 * r + k], h_r.at[32 + 2 * r + k], node, wrap(y + 1 - 2 * k, Y))

    def h_y_in(r, k):
        ref = yt.at[place_z(r), :, c, :, lanes(others + 128 * k, 128)]
        return push(ref, ref, h_s.at[32 + 2 * r + k], h_r.at[32 + 2 * r + k], sibling, y)

    def h_core(r, k, core):
        ref = yt.at[place_z(r), :, core, :, lanes(mine if k == 0 else others, HALF)]
        return push(ref, ref, h_s.at[48 + 2 * r + k], h_r.at[48 + 2 * r + k], sibling, y)

    for r in range(1, Z):
        f_z(r).start()
    for k in range(X - 1):
        f_x(0, k).start()
    loads["hist"].wait()
    yt[z, x, c, :, lanes(mine, HALF)] = mm_tn(pick, hist[...]).astype(BF16)
    for k in range(X - 1):
        l_x(k).start()
    for r in range(1, Z):
        h_z(r).start()
    for k in range(X - 1):
        h_x(0, k).start()

    id_copies = [
        push(ids_all.at[y], ids_all.at[y], id_s.at[d - 1], id_r.at[d - 1], node, wrap(y + d, Y))
        for d in range(1, Y)
    ]
    for cp in id_copies:
        cp.start()

    loads["len"].wait()
    loads["halo"].wait()
    slot = lax.broadcasted_iota(jnp.int32, (HP, Z * GROUP), 0)
    asked = jnp.where(slot < lens[...], halo[...], -1).astype(F32).astype(BF16)
    repeat = jnp.where(
        lax.rem(lax.broadcasted_iota(jnp.int32, (HP, SLOTS), 1), HP) == lax.broadcasted_iota(jnp.int32, (HP, SLOTS), 0),
        1.0, 0.0,
    ).astype(BF16)
    tiled = mm_tn(asked, repeat)
    in_list = lax.div(lax.broadcasted_iota(jnp.int32, (GROUP, SLOTS), 1), HP) == lax.broadcasted_iota(
        jnp.int32, (GROUP, SLOTS), 0
    )
    r_i = lax.broadcasted_iota(jnp.int32, (COLS, SLOTS), 0)
    s_i = lax.broadcasted_iota(jnp.int32, (COLS, SLOTS), 1)
    target = jnp.where(lax.div(r_i, BND) == lax.div(s_i, HP), lax.rem(r_i, BND), -2).astype(F32)
    loads["inner"].wait()
    degree = 1.0 + jnp.sum(inner[...].astype(F32), axis=1, keepdims=True)
    loads["edges"].wait()
    for g in range(Z):
        wanted = jnp.sum(jnp.where(in_list, tiled[g * GROUP:(g + 1) * GROUP], 0.0), axis=0, keepdims=True)
        spread = jnp.where(wanted == target, 1.0, 0.0).astype(BF16)
        part = mm_nt(edges[:, g * SLOTS:(g + 1) * SLOTS], spread)
        degree = degree + jnp.sum(part, axis=1, keepdims=True)
        e[g] = part.astype(BF16)
        e_t[g] = mm_nt(spread, edges[:, g * SLOTS:(g + 1) * SLOTS]).astype(BF16)
    scale = (1.0 - RESIDUAL_SHARE) / degree

    row_of = lax.broadcasted_iota(jnp.int32, (ROWS, TOK), 0)
    place = jnp.where(row_of == ids[...], 1.0, 0.0).astype(BF16)
    x_own = mm_tn(place, feat[...]).astype(BF16)
    loads["w0"].wait()
    h_own, slope_own = gelu_slope(mm(x_own, w0[...]))
    h_own = h_own.astype(BF16)
    own = h_own.astype(F32)
    mix = mm(inner[...], h_own) + own

    for r in range(1, Z):
        f_z_in(r).wait_recv()
        for k in range(X - 1):
            f_x(r, k).start()

    def history_x(r):
        h_z_in(r).wait_recv()
        for k in range(X - 1):
            h_x(r, k).start()

    def features_core(r):
        for k in range(X - 1):
            f_x_in(r, k).wait_recv()
        f_core(r, c).start()

    def history_y(r):
        for k in range(X - 1):
            h_x_in(r, k).wait_recv()
        if r > 0:
            l_z_in(r).wait_recv()
        h_y(r, 0).start()
        h_y(r, 1).start()
        h_core(r, 0, c).start()

    def history_core(r):
        h_y_in(r, 0).wait_recv()
        h_y_in(r, 1).wait_recv()
        h_core(r, 1, c).start()

    def layer_one(r, total):
        f_core(r, 1 - c).wait_recv()
        g = place_z(r)
        h, slope_h = gelu_slope(mm(xt[g].reshape(COLS, FEAT), w0[...]))
        slope[g] = slope_h
        return total + mm(e[g], h.astype(BF16))

    for k in range(X - 1):
        l_x_in(k).wait_recv()
    for r in range(1, Z):
        l_z(r).start()

    for step, r in (
        (history_x, 1), (history_x, 2), (history_x, 3), (features_core, 0), (history_y, 0), (features_core, 1),
        (features_core, 2), (layer_one, 0), (history_x, 4), (history_x, 5), (features_core, 3), (features_core, 4),
        (layer_one, 1), (history_x, 6), (history_x, 7), (features_core, 5), (features_core, 6), (features_core, 7),
        (history_y, 1), (layer_one, 2), (history_y, 2), (layer_one, 3), (history_y, 3), (history_y, 4),
        (layer_one, 4), (history_y, 5), (history_core, 0), (layer_one, 5), (history_y, 6), (history_core, 1),
        (layer_one, 6), (history_y, 7), (history_core, 2), (layer_one, 7), (history_core, 3),
    ):
        if step is layer_one:
            mix = layer_one(r, mix)
        else:
            step(r)
    s1 = (mix * scale + RESIDUAL_SHARE * own).astype(BF16)
    loads["w1"].wait()
    z1 = (1.0 - BETA_ONE) * s1.astype(F32) + BETA_ONE * mm(s1, w1[...])
    fresh, slope_one = gelu_slope(z1)
    fresh = fresh.astype(BF16)

    fresh_all[y] = fresh
    fresh_sent = []

    def fresh_copy(dy, idx, to, half=None):
        block = wrap(y + dy, Y)
        ref = fresh_all.at[block] if half is None else fresh_all.at[block, half * 64:half * 64 + 64]
        return push(ref, ref, fr_s.at[idx], fr_r.at[idx], node, wrap(y + to, Y))

    def fresh_send(*args):
        cp = fresh_copy(*args)
        cp.start()
        fresh_sent.append(cp)

    for step, r in (
        (history_core, 4), (history_core, 5), (history_core, 6), (history_core, 7),
    ):
        step(r)

    fresh_send(0, 2, 2)
    fresh_send(0, 3, -2)
    fresh_send(0, 0, 1)
    fresh_send(0, 1, -1)

    def fresh_pass():
        fresh_copy(-2, 2, 1).wait_recv()
        fresh_copy(2, 3, 1).wait_recv()
        fresh_send(-2, 6, 2, 0)
        fresh_send(2, 7, -2, 1)
        fresh_send(-2, 4, 1)
        fresh_send(2, 5, -1)

    def fresh_end():
        fresh_copy(-3, 4, 1).wait_recv()
        fresh_copy(3, 5, 1).wait_recv()
        fresh_copy(-4, 6, 1, 0).wait_recv()
        fresh_copy(4, 7, 1, 1).wait_recv()

    mix = mm(inner[...], fresh) + fresh.astype(F32)

    for g in range(Z):
        x_t[g] = xt[g].reshape(COLS, FEAT).T
    for r in range(Z):
        h_core(r, 0, 1 - c).wait_recv()
        h_core(r, 1, 1 - c).wait_recv()
        g = place_z(r)
        mix = mix + mm(e[g], yt[g].reshape(COLS, D))
    s2 = (mix * scale + RESIDUAL_SHARE * own).astype(BF16)
    loads["w2"].wait()
    z2 = (1.0 - BETA_TWO) * s2.astype(F32) + BETA_TWO * mm(s2, w2[...])
    _, slope_two = gelu_slope(z2)
    loads["cot"].wait()
    g2 = cot[...].astype(F32) * slope_two
    g2b = g2.astype(BF16)

    def term_start(m, s, gb, beta):
        gh[0] = gb[:, :HALF]
        gh[1] = gb[:, HALF:]
        tsend[m] = (beta * mm_tn(s, gh[1 - c])).astype(BF16).reshape(Z, X, 16, HALF)
        cp = push(tsend.at[m], tcore.at[m], rs_s.at[m, 0], rs_r.at[m, 0], sibling, y)
        cp.start()
        tmine[m] = (beta * mm_tn(s, gh[c])).reshape(Z, X, 16, HALF)
        return cp

    def term_x(m, core_copy):
        core_copy.wait()
        tmine[m] = tmine[m] + tcore[m].astype(F32)
        xsend[m] = tmine[m].astype(BF16)
        copies = []
        for d in range(1, X):
            to = wrap(x + d, X)
            cp = push(xsend.at[m, :, to], xrecv.at[m, d - 1], rs_s.at[m, d], rs_r.at[m, d], node_of(z, to, c), y)
            cp.start()
            copies.append(cp)
        return copies

    def term_z(m, x_copies):
        for cp in x_copies:
            cp.wait()
        total = tmine[m, :, x]
        for d in range(1, X):
            total = total + xrecv[m, d - 1].astype(F32)
        zown[m] = total
        zsend[m] = total.astype(BF16)
        copies = []
        for d in range(1, Z):
            to = wrap(z + d, Z)
            cp = push(
                zsend.at[m, to], zrecv.at[m, d - 1], rs_s.at[m, 3 + d], rs_r.at[m, 3 + d], node_of(to, x, c), y
            )
            cp.start()
            copies.append(cp)
        return copies

    def term_done(m, z_copies):
        for cp in z_copies:
            cp.wait()
        total = zown[m, z]
        for d in range(1, Z):
            total = total + zrecv[m, d - 1].astype(F32)
        return total

    two = term_start(1, s2, g2b, BETA_TWO)
    e2 = (1.0 - BETA_TWO) * g2 + BETA_TWO * mm_nt(g2b, w2[...])
    m2 = (e2 * scale).astype(BF16)
    g1 = (m2.astype(F32) + mm_tn(inner[...], m2)) * slope_one
    g1b = g1.astype(BF16)
    two = term_x(1, two)
    one = term_start(0, s1, g1b, BETA_ONE)
    e1 = (1.0 - BETA_ONE) * g1 + BETA_ONE * mm_nt(g1b, w1[...])
    m1 = (e1 * scale).astype(BF16)
    back_own = RESIDUAL_SHARE * (e1 + e2) + m1.astype(F32) + mm_tn(inner[...], m1)
    q_own = (back_own * slope_own).astype(BF16)
    one = term_x(0, one)

    t0 = mm_tn(x_own, q_own)
    for g in range(Z):
        q = (mm(e_t[g], m1) * slope[g]).astype(BF16)
        t0 = t0 + mm(x_t[g], q)
    qacc[0] = t0[:, :HALF]
    qacc[1] = t0[:, HALF:]

    qsend[...] = qacc[1 - c].astype(BF16)
    q_core = push(qsend, qcore, qs_s.at[0], qs_r.at[0], sibling, y)
    q_core.start()
    fresh_pass()
    two = term_z(1, two)
    q_core.wait()
    total = (qacc[c] + qcore[...].astype(F32)).reshape(Z, 16, HALF)
    qown[...] = total
    qzsend[...] = total.astype(BF16)
    q_z = []
    for d in range(1, Z):
        to = wrap(z + d, Z)
        cp = push(qzsend.at[to], qzrecv.at[d - 1], qs_s.at[d], qs_r.at[d], node_of(to, x, c), y)
        cp.start()
        q_z.append(cp)
    one = term_z(0, one)
    r2 = term_done(1, two)
    fresh_copy(-1, 0, 1).wait_recv()
    fresh_copy(1, 1, 1).wait_recv()
    for cp in id_copies:
        cp.wait()

    def put_rows(blocks):
        at = [wrap(y + d, Y) for d in blocks]
        put = jnp.concatenate([jnp.where(row_of == ids_all[b, 0:1], 1.0, 0.0).astype(BF16) for b in at], axis=1)
        return mm(put, jnp.concatenate([fresh_all[b] for b in at], axis=0))

    new_hist[...] = put_rows((0, -1, 1, -2, 2)).astype(BF16)
    for cp in q_z:
        cp.wait()
    total = qown[z]
    for d in range(1, Z):
        total = total + qzrecv[d - 1].astype(F32)
    qx[...] = total
    q_x = []
    for d in range(1, X):
        cp = push(qx, qxrecv.at[d - 1], qs_s.at[7 + d], qs_r.at[7 + d], node_of(z, wrap(x + d, X), c), y)
        cp.start()
        q_x.append(cp)
    r1 = term_done(0, one)
    for cp in q_x:
        cp.wait()
    r0 = qx[...]
    for d in range(1, X):
        r0 = r0 + qxrecv[d - 1]

    def columns(r, j):
        part = r[:, (j // 2) * 128:(j // 2) * 128 + 128]
        return part if j % 2 == 0 else pltpu.roll(part, 64, 1)

    per_core = Y // C
    me_y = lax.div(y, per_core)
    for j in range(per_core):
        a1, a2, a0 = columns(r1, j), columns(r2, j), columns(r0, j)
        for cc in range(C):
            ysend[j, cc, 0:8] = a1[cc * 8:cc * 8 + 8]
            ysend[j, cc, 8:16] = a2[cc * 8:cc * 8 + 8]
            ysend[j, cc, 16:24] = pltpu.roll(a0, lax.rem(16 - (x * 4 + cc * 2), 16), 0)[0:8]

    def y_copy(j, cc):
        return push(
            ysend.at[j, cc], yrecv.at[y], y_s.at[j * C + cc], y_r.at[y], node_of(z, x, cc), c * per_core + j
        )

    for j in range(per_core):
        for cc in range(C):
            kept = (c * per_core + j == y) & (c == cc)

            @pl.when(jnp.logical_not(kept))
            def _():
                y_copy(j, cc).start()

            @pl.when(kept)
            def _():
                yrecv[y] = ysend[j, cc]

    fresh_end()
    new_hist[...] = (new_hist[...].astype(F32) + put_rows((-3, 3, 4))).astype(BF16)

    for yy in range(Y):
        @pl.when(jnp.logical_not((yy == y) & (me_y == c)))
        def _():
            push(
                ysend.at[0, 0], yrecv.at[yy], y_s.at[0], y_r.at[yy], node, wrap(y + 1, Y)
            ).wait_recv()
    total = yrecv[0]
    for yy in range(1, Y):
        total = total + yrecv[yy]
    total = total * ((Z * X * C * Y) ** (-0.5))
    out1[...] = total[0:8, 0:64]
    out2[...] = total[8:16, 0:64]
    out0[...] = total[16:18, 0:64]

    for cp in fresh_sent:
        cp.wait_send()

    def gather_sent(r, carry):
        for k in range(X - 1):
            f_x(r, k).wait_send()
            h_x(r, k).wait_send()
        f_core(r, c).wait_send()
        for k in range(2):
            h_y(r, k).wait_send()
            h_core(r, k, c).wait_send()
        return carry

    lax.fori_loop(0, Z, gather_sent, 0)
    for r in range(1, Z):
        f_z(r).wait_send()
        h_z(r).wait_send()
        l_z(r).wait_send()
    for k in range(X - 1):
        l_x(k).wait_send()
    for j in range(per_core):
        for cc in range(C):
            kept = (c * per_core + j == y) & (c == cc)

            @pl.when(jnp.logical_not(kept))
            def _():
                y_copy(j, cc).wait_send()


def write_out(a, b, c, d, a_out, b_out, c_out, d_out, sems):
    pairs = [(b, b_out), (c, c_out), (d, d_out)]
    pairs += [(a.at[n * TOK:(n + 1) * TOK], a_out.at[n * TOK:(n + 1) * TOK]) for n in range(Y)]
    copies = [pltpu.make_async_copy(src, dst, sems.at[n]) for n, (src, dst) in enumerate(pairs)]
    for cp in copies:
        cp.start()
    for cp in copies:
        cp.wait()


def per_device(
    features, history, boundary, batch_ids, halo_ids, halo_len, edges_inner, edges_halo,
    input_weight, weight_one, weight_two, cotangent,
):
    vmem = pl.BlockSpec(memory_space=pltpu.VMEM)
    anywhere = pl.BlockSpec(memory_space=pl.ANY)
    dma = pltpu.SemaphoreType.DMA
    results = (
        jax.ShapeDtypeStruct((ROWS, D), BF16),
        jax.ShapeDtypeStruct((2, 64), F32),
        jax.ShapeDtypeStruct((8, 64), F32),
        jax.ShapeDtypeStruct((8, 64), F32),
    )
    outs = pl.pallas_call(
        kernel,
        out_shape=results,
        in_specs=[anywhere] * 12,
        out_specs=(vmem,) * 4,
        scratch_shapes=[
            pltpu.VMEM((ROWS, FEAT), BF16),
            pltpu.VMEM((ROWS, HALF), BF16),
            pltpu.VMEM((BND,), jnp.int32),
            pltpu.VMEM((1, TOK), jnp.int32),
            pltpu.VMEM((HP, Z * GROUP), jnp.int32),
            pltpu.VMEM((1, Z * GROUP), jnp.int32),
            pltpu.VMEM((TOK, TOK), BF16),
            pltpu.VMEM((TOK, Z * SLOTS), BF16),
            pltpu.VMEM((FEAT, D), BF16),
            pltpu.VMEM((D, D), BF16),
            pltpu.VMEM((D, D), BF16),
            pltpu.VMEM((TOK, D), BF16),
            pltpu.VMEM((Z, X, C, BND, FEAT), BF16),
            pltpu.VMEM((Z, X, C, BND, D), BF16),
            pltpu.VMEM((Z, TOK, COLS), BF16),
            pltpu.VMEM((Z, COLS, TOK), BF16),
            pltpu.VMEM((Z, FEAT, COLS), BF16),
            pltpu.VMEM((Z, COLS, D), F32),
            pltpu.VMEM((Y, TOK, D), BF16),
            pltpu.VMEM((Y, 8, TOK), jnp.int32),
            pltpu.VMEM((2, TOK, HALF), BF16),
            pltpu.VMEM((2, Z, X, 16, HALF), F32),
            pltpu.VMEM((2, Z, X, 16, HALF), BF16),
            pltpu.VMEM((2, Z, X, 16, HALF), BF16),
            pltpu.VMEM((2, Z, X, 16, HALF), BF16),
            pltpu.VMEM((2, X - 1, Z, 16, HALF), BF16),
            pltpu.VMEM((2, Z, 16, HALF), F32),
            pltpu.VMEM((2, Z, 16, HALF), BF16),
            pltpu.VMEM((2, Z - 1, 16, HALF), BF16),
            pltpu.VMEM((2, FEAT, HALF), F32),
            pltpu.VMEM((FEAT, HALF), BF16),
            pltpu.VMEM((FEAT, HALF), BF16),
            pltpu.VMEM((Z, 16, HALF), F32),
            pltpu.VMEM((Z, 16, HALF), BF16),
            pltpu.VMEM((Z - 1, 16, HALF), BF16),
            pltpu.VMEM((16, HALF), F32),
            pltpu.VMEM((X - 1, 16, HALF), F32),
            pltpu.VMEM((Y // C, C, 24, 128), F32),
            pltpu.VMEM((Y, 24, 128), F32),
            dma((12,)),
            dma((40,)),
            dma((40,)),
            dma((75,)),
            dma((75,)),
            dma((8,)),
            dma((8,)),
            dma((Y - 1,)),
            dma((Y - 1,)),
            dma((2, 11)),
            dma((2, 11)),
            dma((11,)),
            dma((11,)),
            dma((8,)),
            dma((8,)),
        ],
        compiler_params=pltpu.CompilerParams(
            collective_id=0, has_side_effects=True, vmem_limit_bytes=62 * 1024 * 1024
        ),
        name="gcn_step",
    )(
        features, history, boundary, batch_ids, jnp.swapaxes(halo_ids, 2, 3), halo_len, edges_inner, edges_halo,
        input_weight, weight_one, weight_two, cotangent,
    )
    return pl.pallas_call(
        write_out,
        out_shape=results,
        in_specs=[vmem] * 4,
        out_specs=(anywhere,) * 4,
        scratch_shapes=[dma((3 + Y,))],
        name="write_out",
    )(*outs)


def solution(mesh):
    return jax.shard_map(
        per_device,
        mesh=mesh,
        in_specs=(
            P("node", None),
            P("node", None),
            P("node"),
            P("node", "dp", None),
            P("node", "dp", None, None),
            P("node", "dp", None),
            P("node", "dp", None, None),
            P("node", "dp", None, None),
            P(),
            P(),
            P(),
            P("node", "dp", None, None),
        ),
        out_specs=(P("node", None), P("node", "dp"), P("node", "dp"), P("node", "dp")),
        check_vma=False,
    )
```

```python
import math

import jax
import jax.numpy as jnp
from jax import lax
from jax.experimental import pallas as pl
from jax.experimental.pallas import tpu as pltpu
from jax.sharding import PartitionSpec as P

RESIDUAL_SHARE = 0.1
BETA_ONE = math.log(1.5)
BETA_TWO = math.log(1.25)
GELU_SCALE = math.sqrt(2.0 / math.pi)
CUBIC_TERM = 0.044715

Z, X, C, Y = 8, 4, 2, 8
D, FEAT, TOK, HP, BND, ROWS = 512, 128, 128, 32, 48, 1024
HALF = D // 2
GROUP = X * C
COLS = GROUP * BND
SLOTS = GROUP * HP

FIRST, LAST = pl.ds(0, 32), pl.ds(32, 16)

F32 = jnp.float32
BF16 = jnp.bfloat16


def gelu(v):
    vv = v * v
    half = 0.5 + 0.5 * jnp.tanh(v * (GELU_SCALE + (GELU_SCALE * CUBIC_TERM) * vv))
    return v * half


def gelu_slope(v):
    vv = v * v
    half = 0.5 + 0.5 * jnp.tanh(v * (GELU_SCALE + (GELU_SCALE * CUBIC_TERM) * vv))
    g = v * half
    rise = (2.0 * GELU_SCALE) + (6.0 * GELU_SCALE * CUBIC_TERM) * vv
    return g, half + (g * (1.0 - half)) * rise


def mm(a, b):
    return lax.dot_general(a, b, (((1,), (0,)), ((), ())), preferred_element_type=F32)


def mm_tn(a, b):
    return lax.dot_general(a, b, (((0,), (0,)), ((), ())), preferred_element_type=F32)


def mm_nt(a, b):
    return lax.dot_general(a, b, (((1,), (1,)), ((), ())), preferred_element_type=F32)


def kernel(
    feat_in, hist_in, bnd_in, ids_in, halo_in, len_in, inner_in, edges_in, w0_in, w1_in, w2_in, cot_in,
    new_hist, out0, out1, out2,
    feat, hist, bnd, ids, halo, lens, inner, edges, w0, w1, w2, cot,
    xt, yt, e, e_t, x_t, slope, fresh_all, ids_all,
    gh, tmine, tsend, tcore, xsend, xrecv, zown, zsend, zrecv,
    qacc, qsend, qcore, qown, qzsend, qzrecv, qx, qxrecv, ysend, yrecv,
    in_s, f_s, f_r, h_s, h_r, fr_s, fr_r, id_s, id_r, rs_s, rs_r, qs_s, qs_r, y_s, y_r,
):
    node = lax.axis_index("node")
    y = lax.axis_index("dp")
    c = lax.rem(node, C)
    x = lax.rem(lax.div(node, C), X)
    z = lax.div(node, C * X)

    loads = {}
    for n, (name, src, dst) in enumerate((
        ("bnd", bnd_in, bnd), ("feat", feat_in, feat), ("hist", hist_in.at[:, pl.ds(pl.multiple_of(lax.rem(y, 2) * HALF, HALF), HALF)], hist), ("ids", ids_in.at[0], ids),
        ("halo", halo_in.at[0, 0], halo), ("len", len_in.at[0], lens), ("edges", edges_in.at[0, 0], edges),
        ("inner", inner_in.at[0, 0], inner), ("w0", w0_in, w0), ("w1", w1_in, w1), ("w2", w2_in, w2),
        ("cot", cot_in.at[0, 0], cot),
    )):
        loads[name] = pltpu.make_async_copy(src, dst, in_s.at[n])
        loads[name].start()

    def wrap(v, n):
        return lax.rem(v + n, n)

    def node_of(zz, xx, cc):
        return (zz * X + xx) * C + cc

    def push(src, dst, ssem, rsem, to_node, to_y):
        return pltpu.make_async_remote_copy(
            src_ref=src, dst_ref=dst, send_sem=ssem, recv_sem=rsem,
            device_id=(to_node, to_y), device_id_type=pl.DeviceIdType.MESH,
        )

    barrier = pltpu.get_barrier_semaphore()
    far_first = (4, 3, 5, 2, 6, 1, 7)
    peers = [(node_of(wrap(z + d, Z), x, c), y) for d in far_first]
    peers += [(node_of(z, x, cc), wrap(y + d, Y)) for d in far_first for cc in range(C)]
    peers += [(node_of(z, wrap(x + d, X), c), y) for d in (2, 1, 3)]
    peers += [(node_of(z, x, 1 - c), y)]
    for to_node, to_y in peers:
        pl.semaphore_signal(barrier, inc=1, device_id=(to_node, to_y), device_id_type=pl.DeviceIdType.MESH)

    side = lax.rem(y, 2)

    def lanes(start, size):
        return pl.ds(pl.multiple_of(start, 128), size)

    mine, others = side * HALF, (1 - side) * HALF
    row_of = lax.broadcasted_iota(jnp.int32, (ROWS, BND), 0)
    loads["bnd"].wait()
    pick = jnp.where(row_of == bnd[...].reshape(1, BND), 1.0, 0.0).astype(BF16)
    loads["feat"].wait()
    xt[z, x, c] = mm_tn(pick, feat[...]).astype(BF16)
    loads["ids"].wait()
    ids_all[y] = jnp.broadcast_to(ids[...], (8, TOK))

    pl.semaphore_wait(barrier, len(peers))

    sibling = node_of(z, x, 1 - c)

    def place_z(r, sign=1):
        if isinstance(r, int):
            step = (r + 1) // 2 if r % 2 == 1 else -(r // 2)
        else:
            far = lax.div(r + 1, 2)
            step = jnp.where(lax.rem(r, 2) == 1, far, -far)
        return wrap(z + sign * step, Z)

    def x_peer(k):
        return node_of(z, wrap(x + k + 1, X), c)

    def f_z(r):
        ref = xt.at[z, x, c]
        return push(ref, ref, f_s.at[r], f_r.at[r], node_of(place_z(r, -1), x, c), y)

    def f_z_in(r):
        ref = xt.at[place_z(r), x, c]
        return push(ref, ref, f_s.at[r], f_r.at[r], sibling, y)

    def f_x(r, k):
        ref = xt.at[place_z(r), x, c]
        return push(ref, ref, f_s.at[8 + 3 * r + k], f_r.at[8 + 3 * r + k], x_peer(k), y)

    def f_x_in(r, k):
        ref = xt.at[place_z(r), wrap(x - k - 1, X), c]
        return push(ref, ref, f_s.at[8 + 3 * r + k], f_r.at[8 + 3 * r + k], sibling, y)

    def f_core(r, core):
        ref = xt.at[place_z(r), :, core]
        return push(ref, ref, f_s.at[32 + r], f_r.at[32 + r], sibling, y)

    def h_z(r):
        ref = yt.at[z, x, c, FIRST, lanes(mine, HALF)]
        return push(ref, ref, h_s.at[r], h_r.at[r], node_of(place_z(r, -1), x, c), y)

    def h_z_in(r):
        ref = yt.at[place_z(r), x, c, FIRST, lanes(mine, HALF)]
        return push(ref, ref, h_s.at[r], h_r.at[r], sibling, y)

    def h_x(r, k):
        ref = yt.at[place_z(r), x, c, FIRST, lanes(mine, HALF)]
        return push(ref, ref, h_s.at[8 + 3 * r + k], h_r.at[8 + 3 * r + k], x_peer(k), y)

    def h_x_in(r, k):
        ref = yt.at[place_z(r), wrap(x - k - 1, X), c, FIRST, lanes(mine, HALF)]
        return push(ref, ref, h_s.at[8 + 3 * r + k], h_r.at[8 + 3 * r + k], sibling, y)

    def l_x(k):
        ref = yt.at[z, x, c, LAST, lanes(mine, HALF)]
        return push(ref, ref, h_s.at[64 + k], h_r.at[64 + k], x_peer(k), y)

    def l_x_in(k):
        ref = yt.at[z, wrap(x - k - 1, X), c, LAST, lanes(mine, HALF)]
        return push(ref, ref, h_s.at[64 + k], h_r.at[64 + k], sibling, y)

    def l_z(r):
        ref = yt.at[z, :, c, LAST, lanes(mine, HALF)]
        return push(ref, ref, h_s.at[67 + r], h_r.at[67 + r], node_of(place_z(r, -1), x, c), y)

    def l_z_in(r):
        ref = yt.at[place_z(r), :, c, LAST, lanes(mine, HALF)]
        return push(ref, ref, h_s.at[67 + r], h_r.at[67 + r], sibling, y)

    def h_y(r, k):
        ref = yt.at[place_z(r), :, c, :, lanes(mine + 128 * k, 128)]
        return push(ref, ref, h_s.at[32 + 2 * r + k], h_r.at[32 + 2 * r + k], node, wrap(y + 1 - 2 * k, Y))

    def h_y_in(r, k):
        ref = yt.at[place_z(r), :, c, :, lanes(others + 128 * k, 128)]
        return push(ref, ref, h_s.at[32 + 2 * r + k], h_r.at[32 + 2 * r + k], sibling, y)

    def h_core(r, k, core):
        ref = yt.at[place_z(r), :, core, :, lanes(mine if k == 0 else others, HALF)]
        return push(ref, ref, h_s.at[48 + 2 * r + k], h_r.at[48 + 2 * r + k], sibling, y)

    for r in range(1, Z):
        f_z(r).start()
    for k in range(X - 1):
        f_x(0, k).start()
    loads["hist"].wait()
    yt[z, x, c, :, lanes(mine, HALF)] = mm_tn(pick, hist[...]).astype(BF16)
    for k in range(X - 1):
        l_x(k).start()
    for r in range(1, Z):
        h_z(r).start()
    for k in range(X - 1):
        h_x(0, k).start()

    id_copies = [
        push(ids_all.at[y], ids_all.at[y], id_s.at[d - 1], id_r.at[d - 1], node, wrap(y + d, Y))
        for d in range(1, Y)
    ]
    for cp in id_copies:
        cp.start()

    loads["len"].wait()
    loads["halo"].wait()
    slot = lax.broadcasted_iota(jnp.int32, (HP, Z * GROUP), 0)
    asked = jnp.where(slot < lens[...], halo[...], -1).astype(F32).astype(BF16)
    repeat = jnp.where(
        lax.rem(lax.broadcasted_iota(jnp.int32, (HP, SLOTS), 1), HP) == lax.broadcasted_iota(jnp.int32, (HP, SLOTS), 0),
        1.0, 0.0,
    ).astype(BF16)
    tiled = mm_tn(asked, repeat)
    in_list = lax.div(lax.broadcasted_iota(jnp.int32, (GROUP, SLOTS), 1), HP) == lax.broadcasted_iota(
        jnp.int32, (GROUP, SLOTS), 0
    )
    r_i = lax.broadcasted_iota(jnp.int32, (COLS, SLOTS), 0)
    s_i = lax.broadcasted_iota(jnp.int32, (COLS, SLOTS), 1)
    target = jnp.where(lax.div(r_i, BND) == lax.div(s_i, HP), lax.rem(r_i, BND), -2).astype(F32)
    loads["inner"].wait()
    degree = 1.0 + jnp.sum(inner[...].astype(F32), axis=1, keepdims=True)
    loads["edges"].wait()
    for g in range(Z):
        wanted = jnp.sum(jnp.where(in_list, tiled[g * GROUP:(g + 1) * GROUP], 0.0), axis=0, keepdims=True)
        spread = jnp.where(wanted == target, 1.0, 0.0).astype(BF16)
        part = mm_nt(edges[:, g * SLOTS:(g + 1) * SLOTS], spread)
        degree = degree + jnp.sum(part, axis=1, keepdims=True)
        e[g] = part.astype(BF16)
        e_t[g] = mm_nt(spread, edges[:, g * SLOTS:(g + 1) * SLOTS]).astype(BF16)
    scale = (1.0 - RESIDUAL_SHARE) / degree

    row_of = lax.broadcasted_iota(jnp.int32, (ROWS, TOK), 0)
    place = jnp.where(row_of == ids[...], 1.0, 0.0).astype(BF16)
    x_own = mm_tn(place, feat[...]).astype(BF16)
    loads["w0"].wait()
    h_own, slope_own = gelu_slope(mm(x_own, w0[...]))
    h_own = h_own.astype(BF16)
    own = h_own.astype(F32)
    mix = mm(inner[...], h_own) + own

    for r in range(1, Z):
        f_z_in(r).wait_recv()
        for k in range(X - 1):
            f_x(r, k).start()

    def history_x(r):
        h_z_in(r).wait_recv()
        for k in range(X - 1):
            h_x(r, k).start()

    def features_core(r):
        for k in range(X - 1):
            f_x_in(r, k).wait_recv()
        f_core(r, c).start()

    def history_y(r):
        for k in range(X - 1):
            h_x_in(r, k).wait_recv()
        if r > 0:
            l_z_in(r).wait_recv()
        h_y(r, 0).start()
        h_y(r, 1).start()
        h_core(r, 0, c).start()

    def history_core(r):
        h_y_in(r, 0).wait_recv()
        h_y_in(r, 1).wait_recv()
        h_core(r, 1, c).start()

    def layer_one(r, total):
        f_core(r, 1 - c).wait_recv()
        g = place_z(r)
        h, slope_h = gelu_slope(mm(xt[g].reshape(COLS, FEAT), w0[...]))
        slope[g] = slope_h
        return total + mm(e[g], h.astype(BF16))

    for k in range(X - 1):
        l_x_in(k).wait_recv()
    for r in range(1, Z):
        l_z(r).start()

    for step, r in (
        (history_x, 1), (history_x, 2), (history_x, 3), (features_core, 0), (history_y, 0), (features_core, 1),
        (features_core, 2), (layer_one, 0), (history_x, 4), (history_x, 5), (features_core, 3), (features_core, 4),
        (layer_one, 1), (history_x, 6), (history_x, 7), (features_core, 5), (features_core, 6), (features_core, 7),
        (history_y, 1), (layer_one, 2), (history_y, 2), (layer_one, 3), (history_y, 3), (history_y, 4),
        (layer_one, 4), (history_y, 5), (history_core, 0), (layer_one, 5), (history_y, 6), (history_core, 1),
        (layer_one, 6), (history_y, 7), (history_core, 2), (layer_one, 7), (history_core, 3),
    ):
        if step is layer_one:
            mix = layer_one(r, mix)
        else:
            step(r)
    s1 = (mix * scale + RESIDUAL_SHARE * own).astype(BF16)
    loads["w1"].wait()
    z1 = (1.0 - BETA_ONE) * s1.astype(F32) + BETA_ONE * mm(s1, w1[...])
    fresh, slope_one = gelu_slope(z1)
    fresh = fresh.astype(BF16)

    fresh_all[y] = fresh
    fresh_sent = []

    def fresh_copy(dy, idx, to, half=None):
        block = wrap(y + dy, Y)
        ref = fresh_all.at[block] if half is None else fresh_all.at[block, half * 64:half * 64 + 64]
        return push(ref, ref, fr_s.at[idx], fr_r.at[idx], node, wrap(y + to, Y))

    def fresh_send(*args):
        cp = fresh_copy(*args)
        cp.start()
        fresh_sent.append(cp)

    for step, r in (
        (history_core, 4), (history_core, 5), (history_core, 6), (history_core, 7),
    ):
        step(r)

    fresh_send(0, 2, 2)
    fresh_send(0, 3, -2)
    fresh_send(0, 0, 1)
    fresh_send(0, 1, -1)

    def fresh_pass():
        fresh_copy(-2, 2, 1).wait_recv()
        fresh_copy(2, 3, 1).wait_recv()
        fresh_send(-2, 6, 2, 0)
        fresh_send(2, 7, -2, 1)
        fresh_send(-2, 4, 1)
        fresh_send(2, 5, -1)

    def fresh_end():
        fresh_copy(-3, 4, 1).wait_recv()
        fresh_copy(3, 5, 1).wait_recv()
        fresh_copy(-4, 6, 1, 0).wait_recv()
        fresh_copy(4, 7, 1, 1).wait_recv()

    mix = mm(inner[...], fresh) + fresh.astype(F32)

    for g in range(Z):
        x_t[g] = xt[g].reshape(COLS, FEAT).T
    for r in range(Z):
        h_core(r, 0, 1 - c).wait_recv()
        h_core(r, 1, 1 - c).wait_recv()
        g = place_z(r)
        mix = mix + mm(e[g], yt[g].reshape(COLS, D))
    s2 = (mix * scale + RESIDUAL_SHARE * own).astype(BF16)
    loads["w2"].wait()
    z2 = (1.0 - BETA_TWO) * s2.astype(F32) + BETA_TWO * mm(s2, w2[...])
    _, slope_two = gelu_slope(z2)
    loads["cot"].wait()
    g2 = cot[...].astype(F32) * slope_two
    g2b = g2.astype(BF16)

    def term_start(m, s, gb, beta):
        gh[0] = gb[:, :HALF]
        gh[1] = gb[:, HALF:]
        tsend[m] = (beta * mm_tn(s, gh[1 - c])).astype(BF16).reshape(Z, X, 16, HALF)
        cp = push(tsend.at[m], tcore.at[m], rs_s.at[m, 0], rs_r.at[m, 0], sibling, y)
        cp.start()
        tmine[m] = (beta * mm_tn(s, gh[c])).reshape(Z, X, 16, HALF)
        return cp

    def term_x(m, core_copy):
        core_copy.wait()
        tmine[m] = tmine[m] + tcore[m].astype(F32)
        xsend[m] = tmine[m].astype(BF16)
        copies = []
        for d in range(1, X):
            to = wrap(x + d, X)
            cp = push(xsend.at[m, :, to], xrecv.at[m, d - 1], rs_s.at[m, d], rs_r.at[m, d], node_of(z, to, c), y)
            cp.start()
            copies.append(cp)
        return copies

    def term_z(m, x_copies):
        for cp in x_copies:
            cp.wait()
        total = tmine[m, :, x]
        for d in range(1, X):
            total = total + xrecv[m, d - 1].astype(F32)
        zown[m] = total
        zsend[m] = total.astype(BF16)
        copies = []
        for d in range(1, Z):
            to = wrap(z + d, Z)
            cp = push(
                zsend.at[m, to], zrecv.at[m, d - 1], rs_s.at[m, 3 + d], rs_r.at[m, 3 + d], node_of(to, x, c), y
            )
            cp.start()
            copies.append(cp)
        return copies

    def term_done(m, z_copies):
        for cp in z_copies:
            cp.wait()
        total = zown[m, z]
        for d in range(1, Z):
            total = total + zrecv[m, d - 1].astype(F32)
        return total

    two = term_start(1, s2, g2b, BETA_TWO)
    e2 = (1.0 - BETA_TWO) * g2 + BETA_TWO * mm_nt(g2b, w2[...])
    m2 = (e2 * scale).astype(BF16)
    g1 = (m2.astype(F32) + mm_tn(inner[...], m2)) * slope_one
    g1b = g1.astype(BF16)
    two = term_x(1, two)
    one = term_start(0, s1, g1b, BETA_ONE)
    e1 = (1.0 - BETA_ONE) * g1 + BETA_ONE * mm_nt(g1b, w1[...])
    m1 = (e1 * scale).astype(BF16)
    back_own = RESIDUAL_SHARE * (e1 + e2) + m1.astype(F32) + mm_tn(inner[...], m1)
    q_own = (back_own * slope_own).astype(BF16)
    one = term_x(0, one)

    t0 = mm_tn(x_own, q_own)
    for g in range(Z):
        q = (mm(e_t[g], m1) * slope[g]).astype(BF16)
        t0 = t0 + mm(x_t[g], q)
    qacc[0] = t0[:, :HALF]
    qacc[1] = t0[:, HALF:]

    qsend[...] = qacc[1 - c].astype(BF16)
    q_core = push(qsend, qcore, qs_s.at[0], qs_r.at[0], sibling, y)
    q_core.start()
    fresh_pass()
    two = term_z(1, two)
    q_core.wait()
    total = (qacc[c] + qcore[...].astype(F32)).reshape(Z, 16, HALF)
    qown[...] = total
    qzsend[...] = total.astype(BF16)
    q_z = []
    for d in range(1, Z):
        to = wrap(z + d, Z)
        cp = push(qzsend.at[to], qzrecv.at[d - 1], qs_s.at[d], qs_r.at[d], node_of(to, x, c), y)
        cp.start()
        q_z.append(cp)
    one = term_z(0, one)
    r2 = term_done(1, two)
    fresh_copy(-1, 0, 1).wait_recv()
    fresh_copy(1, 1, 1).wait_recv()
    for cp in id_copies:
        cp.wait()

    def put_rows(blocks):
        at = [wrap(y + d, Y) for d in blocks]
        put = jnp.concatenate([jnp.where(row_of == ids_all[b, 0:1], 1.0, 0.0).astype(BF16) for b in at], axis=1)
        return mm(put, jnp.concatenate([fresh_all[b] for b in at], axis=0))

    new_hist[...] = put_rows((0, -1, 1, -2, 2)).astype(BF16)

    def gather_sent(r, carry):
        for k in range(X - 1):
            f_x(r, k).wait_send()
            h_x(r, k).wait_send()
        f_core(r, c).wait_send()
        for k in range(2):
            h_y(r, k).wait_send()
            h_core(r, k, c).wait_send()
        return carry

    lax.fori_loop(0, Z, gather_sent, 0)
    for r in range(1, Z):
        f_z(r).wait_send()
        h_z(r).wait_send()
        l_z(r).wait_send()
    for k in range(X - 1):
        l_x(k).wait_send()

    for cp in q_z:
        cp.wait()
    total = qown[z]
    for d in range(1, Z):
        total = total + qzrecv[d - 1].astype(F32)
    qx[...] = total
    q_x = []
    for d in range(1, X):
        cp = push(qx, qxrecv.at[d - 1], qs_s.at[7 + d], qs_r.at[7 + d], node_of(z, wrap(x + d, X), c), y)
        cp.start()
        q_x.append(cp)
    r1 = term_done(0, one)
    for cp in q_x:
        cp.wait()
    r0 = qx[...]
    for d in range(1, X):
        r0 = r0 + qxrecv[d - 1]

    def columns(r, j):
        part = r[:, (j // 2) * 128:(j // 2) * 128 + 128]
        return part if j % 2 == 0 else pltpu.roll(part, 64, 1)

    per_core = Y // C
    me_y = lax.div(y, per_core)
    for j in range(per_core):
        a1, a2, a0 = columns(r1, j), columns(r2, j), columns(r0, j)
        for cc in range(C):
            ysend[j, cc, 0:8] = a1[cc * 8:cc * 8 + 8]
            ysend[j, cc, 8:16] = a2[cc * 8:cc * 8 + 8]
            ysend[j, cc, 16:24] = pltpu.roll(a0, lax.rem(16 - (x * 4 + cc * 2), 16), 0)[0:8]

    def y_copy(j, cc):
        return push(
            ysend.at[j, cc], yrecv.at[y], y_s.at[j * C + cc], y_r.at[y], node_of(z, x, cc), c * per_core + j
        )

    for j in range(per_core):
        for cc in range(C):
            kept = (c * per_core + j == y) & (c == cc)

            @pl.when(jnp.logical_not(kept))
            def _():
                y_copy(j, cc).start()

            @pl.when(kept)
            def _():
                yrecv[y] = ysend[j, cc]

    fresh_end()
    new_hist[...] = (new_hist[...].astype(F32) + put_rows((-3, 3, 4))).astype(BF16)
    for cp in fresh_sent:
        cp.wait_send()

    for yy in range(Y):
        @pl.when(jnp.logical_not((yy == y) & (me_y == c)))
        def _():
            push(
                ysend.at[0, 0], yrecv.at[yy], y_s.at[0], y_r.at[yy], node, wrap(y + 1, Y)
            ).wait_recv()
    total = yrecv[0]
    for yy in range(1, Y):
        total = total + yrecv[yy]
    total = total * ((Z * X * C * Y) ** (-0.5))
    out1[...] = total[0:8, 0:64]
    out2[...] = total[8:16, 0:64]
    out0[...] = total[16:18, 0:64]


    for j in range(per_core):
        for cc in range(C):
            kept = (c * per_core + j == y) & (c == cc)

            @pl.when(jnp.logical_not(kept))
            def _():
                y_copy(j, cc).wait_send()


def write_out(a, b, c, d, a_out, b_out, c_out, d_out, sems):
    pairs = [(b, b_out), (c, c_out), (d, d_out)]
    pairs += [(a.at[n * TOK:(n + 1) * TOK], a_out.at[n * TOK:(n + 1) * TOK]) for n in range(Y)]
    copies = [pltpu.make_async_copy(src, dst, sems.at[n]) for n, (src, dst) in enumerate(pairs)]
    for cp in copies:
        cp.start()
    for cp in copies:
        cp.wait()


def per_device(
    features, history, boundary, batch_ids, halo_ids, halo_len, edges_inner, edges_halo,
    input_weight, weight_one, weight_two, cotangent,
):
    vmem = pl.BlockSpec(memory_space=pltpu.VMEM)
    anywhere = pl.BlockSpec(memory_space=pl.ANY)
    dma = pltpu.SemaphoreType.DMA
    results = (
        jax.ShapeDtypeStruct((ROWS, D), BF16),
        jax.ShapeDtypeStruct((2, 64), F32),
        jax.ShapeDtypeStruct((8, 64), F32),
        jax.ShapeDtypeStruct((8, 64), F32),
    )
    outs = pl.pallas_call(
        kernel,
        out_shape=results,
        in_specs=[anywhere] * 12,
        out_specs=(vmem,) * 4,
        scratch_shapes=[
            pltpu.VMEM((ROWS, FEAT), BF16),
            pltpu.VMEM((ROWS, HALF), BF16),
            pltpu.VMEM((BND,), jnp.int32),
            pltpu.VMEM((1, TOK), jnp.int32),
            pltpu.VMEM((HP, Z * GROUP), jnp.int32),
            pltpu.VMEM((1, Z * GROUP), jnp.int32),
            pltpu.VMEM((TOK, TOK), BF16),
            pltpu.VMEM((TOK, Z * SLOTS), BF16),
            pltpu.VMEM((FEAT, D), BF16),
            pltpu.VMEM((D, D), BF16),
            pltpu.VMEM((D, D), BF16),
            pltpu.VMEM((TOK, D), BF16),
            pltpu.VMEM((Z, X, C, BND, FEAT), BF16),
            pltpu.VMEM((Z, X, C, BND, D), BF16),
            pltpu.VMEM((Z, TOK, COLS), BF16),
            pltpu.VMEM((Z, COLS, TOK), BF16),
            pltpu.VMEM((Z, FEAT, COLS), BF16),
            pltpu.VMEM((Z, COLS, D), F32),
            pltpu.VMEM((Y, TOK, D), BF16),
            pltpu.VMEM((Y, 8, TOK), jnp.int32),
            pltpu.VMEM((2, TOK, HALF), BF16),
            pltpu.VMEM((2, Z, X, 16, HALF), F32),
            pltpu.VMEM((2, Z, X, 16, HALF), BF16),
            pltpu.VMEM((2, Z, X, 16, HALF), BF16),
            pltpu.VMEM((2, Z, X, 16, HALF), BF16),
            pltpu.VMEM((2, X - 1, Z, 16, HALF), BF16),
            pltpu.VMEM((2, Z, 16, HALF), F32),
            pltpu.VMEM((2, Z, 16, HALF), BF16),
            pltpu.VMEM((2, Z - 1, 16, HALF), BF16),
            pltpu.VMEM((2, FEAT, HALF), F32),
            pltpu.VMEM((FEAT, HALF), BF16),
            pltpu.VMEM((FEAT, HALF), BF16),
            pltpu.VMEM((Z, 16, HALF), F32),
            pltpu.VMEM((Z, 16, HALF), BF16),
            pltpu.VMEM((Z - 1, 16, HALF), BF16),
            pltpu.VMEM((16, HALF), F32),
            pltpu.VMEM((X - 1, 16, HALF), F32),
            pltpu.VMEM((Y // C, C, 24, 128), F32),
            pltpu.VMEM((Y, 24, 128), F32),
            dma((12,)),
            dma((40,)),
            dma((40,)),
            dma((75,)),
            dma((75,)),
            dma((8,)),
            dma((8,)),
            dma((Y - 1,)),
            dma((Y - 1,)),
            dma((2, 11)),
            dma((2, 11)),
            dma((11,)),
            dma((11,)),
            dma((8,)),
            dma((8,)),
        ],
        compiler_params=pltpu.CompilerParams(
            collective_id=0, has_side_effects=True, vmem_limit_bytes=62 * 1024 * 1024
        ),
        name="gcn_step",
    )(
        features, history, boundary, batch_ids, jnp.swapaxes(halo_ids, 2, 3), halo_len, edges_inner, edges_halo,
        input_weight, weight_one, weight_two, cotangent,
    )
    return pl.pallas_call(
        write_out,
        out_shape=results,
        in_specs=[vmem] * 4,
        out_specs=(anywhere,) * 4,
        scratch_shapes=[dma((3 + Y,))],
        name="write_out",
    )(*outs)


def solution(mesh):
    return jax.shard_map(
        per_device,
        mesh=mesh,
        in_specs=(
            P("node", None),
            P("node", None),
            P("node"),
            P("node", "dp", None),
            P("node", "dp", None, None),
            P("node", "dp", None),
            P("node", "dp", None, None),
            P("node", "dp", None, None),
            P(),
            P(),
            P(),
            P("node", "dp", None, None),
        ),
        out_specs=(P("node", None), P("node", "dp"), P("node", "dp"), P("node", "dp")),
        check_vma=False,
    )
```
